32 devices in a mesh: node: 4 (over y, core), rows: 8 (over z, x).
Axes of the slice: x: 2, y: 2, z: 4, core: 2. Of those that a mesh axis runs over, the one named last changes fastest.
Arguments:
- columns: bfloat16 [32, 192, 128], P(None, 'rows'), may hold values from -6 to 6
- pencil_e: bfloat16 [192, 5, 128, 128], P('rows'), may hold values from -2 to 3, as said below
- pencil_a: bfloat16 [192, 5, 128, 128], P('rows'), may hold values from -5 to 2, as said below
- precond: bfloat16 [4, 2, 192, 128, 128], P('node', None, 'rows'), may hold values from -30 to 30, as said below
- neighbours: int32 [192, 5], P('rows'), may hold values from 0 to 191, as said below
Outputs:
- projected: float32 [2, 32, 192, 128], P(None, 'node', 'rows')
The draws below stay inside these ranges and needn't reach their ends.
Inputs may be any that keep to these rules, and one draw needn't show every extreme that they name: neighbours[i, 0] = i. Every entry lies in the block rows of a device whose index along rows is at most 2 away, or exactly half of the 8 devices away, counted around the cycle. For each device and each other device, at most 6 entries of the first one's block rows lie in the second one's block rows; every device has exactly 6 entries in the block rows of the device half the cycle away. `pencil_e`: slot 0 holds the diagonal block. `pencil_a`: slot 0 holds the diagonal block. precond[k, 0, i] + i precond[k, 1, i] is the inverse of z_k E_i - A_i, where E_i and A_i are the float32 diagonal blocks before they were rounded to give pencil_e[i, 0] and pencil_a[i, 0]; the inverse is then rounded to bfloat16.
All inputs are finite; a program needn't handle non-finite values.
Results may differ from the reference program's by a relative error of at most 0.0017.
Values may be sent and summed in bfloat16 or wider, within the bound.
A program may use at most 64 MiB of HBM per device.

```python
import math
import jax
import jax.numpy as jnp
from jax import lax

BS = 128
NCOL = 32
SLOTS = 5
RDEV = 24
HMAX = 6
REACH = 2
SWEEPS = 2
NODES = 4
NBT = 192


def pencil_parts(key):
    subkeys = jax.random.split(jax.random.fold_in(key, 11), 3)
    inside = jax.random.uniform(subkeys[0], (NBT,)) < 0.4
    spread = jax.random.uniform(subkeys[1], (NBT,))
    low_band = jnp.exp(jnp.log(0.05) + spread * (jnp.log(0.2) - jnp.log(0.05)))
    high_band = jnp.exp(jnp.log(1.5) + spread * (jnp.log(3.0) - jnp.log(1.5)))
    shifts = jnp.where(inside, low_band, high_band)
    noise = jax.random.normal(subkeys[2], (2, NBT, SLOTS, BS, BS), jnp.float32) / math.sqrt(BS)
    noise = jnp.clip(noise, -6.0 / math.sqrt(BS), 6.0 / math.sqrt(BS))
    diag_slot = (jnp.arange(SLOTS) == 0).astype(jnp.float32)[None, :, None, None]
    scales = 0.1 + 0.02 * diag_slot
    identity = jnp.eye(BS, dtype=jnp.float32)[None, None]
    matrix_e = noise[0] * scales + diag_slot * identity
    matrix_a = noise[1] * scales - diag_slot * identity * shifts[:, None, None, None]
    return (matrix_e, matrix_a)


def draw_pencil_e(key, part):
    return pencil_parts(key)[0].astype(jnp.bfloat16)


def draw_pencil_a(key, part):
    return pencil_parts(key)[1].astype(jnp.bfloat16)


def draw_precond(key, part):
    matrix_e, matrix_a = pencil_parts(key)
    diag_e = matrix_e[:, 0]
    diag_a = matrix_a[:, 0]

    def per_node(node_index):
        angle_node = 2.0 * math.pi * (node_index.astype(jnp.float32) + 0.5) / NODES
        block_real = jnp.cos(angle_node) * diag_e - diag_a
        block_imag = jnp.sin(angle_node) * diag_e
        upper = jnp.concatenate([block_real, block_imag], axis=2)
        lower = jnp.concatenate([-block_imag, block_real], axis=2)
        inverse = jnp.linalg.inv(jnp.concatenate([upper, lower], axis=1))
        return jnp.stack([inverse[:, :BS, :BS], inverse[:, :BS, BS:]])
    return lax.map(per_node, jnp.arange(NODES)).astype(jnp.bfloat16)


def draw_neighbours(key, part):
    devices = NBT // RDEV
    off_count = (SLOTS - 1) * RDEV
    lanes = 2 * REACH + 1
    dev_keys = jax.random.split(jax.random.fold_in(key, 7), devices)

    def one_device(dev_key, device):
        subkeys = jax.random.split(dev_key, 4)
        lane_order = jax.random.permutation(subkeys[0], lanes)
        counts = jax.random.randint(subkeys[1], (lanes,), 0, HMAX + 1)
        counts = jnp.where(lane_order == 2 * REACH, HMAX, counts)
        bounds = jnp.cumsum(counts)
        position = jnp.arange(off_count)
        which = jnp.sum(position[:, None] >= bounds[None, :], axis=1)
        lane_offset = jnp.where(lane_order < REACH, lane_order - REACH, lane_order - REACH + 1)
        lane_offset = jnp.where(lane_order == 2 * REACH, devices // 2, lane_offset)
        chosen = lane_offset[jnp.minimum(which, lanes - 1)]
        chosen = jnp.where(which < lanes, chosen, 0)
        shuffled = jax.random.permutation(subkeys[2], chosen)
        locals_drawn = jax.random.randint(subkeys[3], (off_count,), 0, RDEV)
        owners = (device + shuffled + devices) % devices
        targets = (owners * RDEV + locals_drawn).reshape(RDEV, SLOTS - 1)
        selves = device * RDEV + jnp.arange(RDEV)
        return jnp.concatenate([selves[:, None], targets], axis=1).astype(jnp.int32)
    blocks = jax.vmap(one_device)(dev_keys, jnp.arange(devices))
    return blocks.reshape(NBT, SLOTS)


def block_levels(stream_key, extent, shards, low, top_value):
    factor_of = 1.0
    for dim, blocks in shards:
        draws = jax.random.uniform(jax.random.fold_in(jax.random.fold_in(stream_key, 6), dim), (blocks,), jnp.float32, low / len(shards), top_value / len(shards))
        factor_of = factor_of * jnp.repeat(jnp.exp(draws), extent[dim] // blocks).reshape((-1,) + (1,) * (len(extent) - 1 - dim))
    return factor_of


def centred(stream_key, shape, deviation, reach, cuts=(), kind=jnp.bfloat16):
    result = deviation * jax.random.normal(stream_key, shape, jnp.float32)
    if cuts:
        result = result * block_levels(stream_key, shape, cuts, -0.22, 0.18)
    return jnp.clip(result, -reach, reach).astype(kind)


def setup_inputs(seed: int = 0) -> dict:
    keys = jax.random.split(jax.random.key(seed), 6)
    columns = centred(keys[0], (NCOL, NBT, BS), 1.0, 6.0, ((1, 8),))
    pencil_e = draw_pencil_e(jax.random.fold_in(keys[5], 71), 0)
    pencil_a = draw_pencil_a(jax.random.fold_in(keys[5], 71), 0)
    precond = draw_precond(jax.random.fold_in(keys[5], 71), 0)
    neighbours = draw_neighbours(jax.random.fold_in(keys[5], 71), 0)
    return {"columns": columns, "pencil_e": pencil_e, "pencil_a": pencil_a, "precond": precond, "neighbours": neighbours}


def apply_blocks(vector, matrices, neighbours):
    summed = jnp.zeros(vector.shape, vector.dtype)
    for slot in range(SLOTS):
        picked = vector[:, neighbours[:, slot], :]
        summed = summed + jnp.einsum('cnb,nbd->cnd', picked, matrices[:, slot])
    return summed

def to_half(value):
    return lax.optimization_barrier(value.astype(jnp.bfloat16)).astype(jnp.float32)

def precondition(residual, inverse):
    products = jnp.einsum('pcnb,mnbd->pmcnd', residual, inverse)
    return jnp.stack([products[0, 0] - products[1, 1], products[0, 1] + products[1, 0]])

def reference(columns, pencil_e, pencil_a, precond, neighbours):
    e_full = pencil_e.astype(jnp.float32)
    a_full = pencil_a.astype(jnp.float32)
    rhs_full = apply_blocks(columns.astype(jnp.float32), e_full, neighbours)
    rhs_round = to_half(rhs_full)
    projected = jnp.zeros((2, NCOL, NBT, BS), jnp.float32)
    for node_index in range(NODES):
        angle_node = 2.0 * math.pi * (node_index + 0.5) / NODES
        node_real = math.cos(angle_node)
        node_imag = math.sin(angle_node)
        inverse = precond[node_index].astype(jnp.float32)
        iterate = jnp.einsum('cnb,mnbd->mcnd', rhs_round, inverse)
        for sweep_step in range(SWEEPS):
            rounded = to_half(iterate).reshape(2 * NCOL, NBT, BS)
            with_e = apply_blocks(rounded, e_full, neighbours).reshape(2, NCOL, NBT, BS)
            with_a = apply_blocks(rounded, a_full, neighbours).reshape(2, NCOL, NBT, BS)
            applied_real = node_real * with_e[0] - node_imag * with_e[1] - with_a[0]
            applied_imag = node_real * with_e[1] + node_imag * with_e[0] - with_a[1]
            residual = to_half(jnp.stack([rhs_full - applied_real, -applied_imag]))
            iterate = iterate + precondition(residual, inverse)
        weighted = jnp.stack([node_real * iterate[0] - node_imag * iterate[1], node_real * iterate[1] + node_imag * iterate[0]])
        projected = projected + weighted / NODES
    return projected
```

```python
import functools
import math

import jax
import jax.numpy as jnp
from jax import lax
from jax.experimental import pallas as pl
from jax.experimental.pallas import tpu as pltpu
from jax.sharding import PartitionSpec as P

SLOTS = 5
HMAX = 6
REACH = 2
SWEEPS = 2
LANES = 2 * REACH + 1
HALO = LANES * HMAX
MESH = pl.DeviceIdType.MESH
ROW_STEP = 4


def lane_offsets(peer_count):
    return list(range(-REACH, 0)) + list(range(1, REACH + 1)) + [peer_count // 2]


def index_tables(neighbours, dev_rows, peer_count):
    my_index = lax.axis_index("rows")
    flat = neighbours.reshape(-1)
    owner = flat // dev_rows
    local = flat - owner * dev_rows
    remote = owner != my_index
    half_cycle = peer_count // 2
    off = (owner - my_index + peer_count) % peer_count
    far = off == half_cycle
    off = jnp.where(off > half_cycle, off - peer_count, off)
    lane = jnp.where(off < 0, off + REACH, off + REACH - 1)
    lane = jnp.where(far, 2 * REACH, lane)
    lane = jnp.where(remote, lane, -1)
    position = jnp.arange(flat.shape[0], dtype=jnp.int32)
    earlier = (lane[None, :] == lane[:, None]) & (position[None, :] < position[:, None])
    rank = jnp.sum(earlier.astype(jnp.int32), axis=1)
    place = jnp.where(remote, lane * HMAX + rank, -1)
    matched = place[None, :] == jnp.arange(HALO, dtype=jnp.int32)[:, None]
    entry = jnp.sum(jnp.where(matched, position[None, :], 0), axis=1)
    wanted = jnp.sum(jnp.where(matched, local[None, :], 0), axis=1)
    own = jnp.where(remote, dev_rows, local)
    arrived = jnp.where(remote, place, HALO)
    table = jnp.concatenate([own, arrived, entry])
    wanted = jnp.pad(wanted.reshape(LANES, 1, HMAX), ((0, 0), (0, 7), (0, 128 - HMAX)))
    return table, wanted


def kernel(
    peer_count,
    node_count,
    table_ref,
    want_ref,
    cols_ref,
    e_ref,
    a_ref,
    p_ref,
    out_ref,
    weights,
    inverse,
    asked_v,
    asked_s,
    send_0,
    send_1,
    send_2,
    halo_0,
    halo_1,
    halo_2,
    vec_1,
    vec_2,
    part_0,
    part,
    prod_0,
    prod,
    rhs,
    iterate,
    share,
    mixed,
    from_core,
    from_y,
    load_sem,
    asked_sem,
    want_send,
    want_recv,
    halo_send,
    halo_recv,
    core_send,
    core_recv,
    y_send,
    y_recv,
):
    dev_rows = rhs.shape[0]
    col_count = rhs.shape[1]
    block = rhs.shape[2]
    entries = dev_rows * SLOTS
    offsets = lane_offsets(peer_count)
    me = lax.axis_index("rows")
    node = lax.axis_index("node")
    y_count = node_count // 2
    my_y = node // 2
    my_core = node % 2
    own_at, arrived_at, entry_at = 0, entries, 2 * entries

    loads = [
        pltpu.make_async_copy(e_ref, weights.at[:, :, 0:block], load_sem.at[0]),
        pltpu.make_async_copy(a_ref, weights.at[:, :, block : 2 * block], load_sem.at[1]),
        pltpu.make_async_copy(p_ref.at[0], inverse.at[:, :, 0:block], load_sem.at[2]),
        pltpu.make_async_copy(p_ref.at[1], inverse.at[:, :, block : 2 * block], load_sem.at[3]),
    ]
    loads[0].start()
    loads[2].start()
    loads[3].start()
    loads[1].start()

    def behind(offset):
        return lax.rem(me + offset + peer_count, peer_count)

    barrier = pltpu.get_barrier_semaphore()
    for offset in offsets:
        pl.semaphore_signal(barrier, inc=1, device_id={"rows": behind(offset)}, device_id_type=MESH)
    for step in range(1, node_count):
        other = lax.rem(node + step, node_count)
        pl.semaphore_signal(barrier, inc=1, device_id={"node": other}, device_id_type=MESH)
    pl.semaphore_wait(barrier, LANES + node_count - 1)

    pending = []
    for lane, offset in enumerate(offsets):
        copy = pltpu.make_async_remote_copy(
            src_ref=want_ref.at[lane],
            dst_ref=asked_v.at[lane],
            send_sem=want_send.at[lane],
            recv_sem=want_recv.at[lane],
            device_id={"rows": behind(offset)},
            device_id_type=MESH,
        )
        copy.start()
        pending.append(copy)

    vec_1[dev_rows] = jnp.zeros(vec_1.shape[1:], vec_1.dtype)
    vec_2[dev_rows] = jnp.zeros(vec_2.shape[1:], vec_2.dtype)
    prod_0[HALO] = jnp.zeros(prod_0.shape[1:], prod_0.dtype)
    prod[HALO] = jnp.zeros(prod.shape[1:], prod.dtype)

    for copy in pending:
        copy.wait_recv()
    to_scalars = pltpu.make_async_copy(asked_v, asked_s, asked_sem)
    to_scalars.start()
    to_scalars.wait()

    lane_order = [LANES - 1] + list(range(LANES - 1))

    def send_halo(phase, vector, outgoing, halo):
        copies = [None] * LANES
        for lane in lane_order:
            for rank in range(HMAX):
                outgoing[lane * HMAX + rank] = vector[asked_s[lane, 0, rank]]
            here = pl.ds(lane * HMAX, HMAX)
            copy = pltpu.make_async_remote_copy(
                src_ref=outgoing.at[here],
                dst_ref=halo.at[here],
                send_sem=halo_send.at[phase, lane],
                recv_sem=halo_recv.at[phase, lane],
                device_id={"rows": behind(-offsets[lane])},
                device_id_type=MESH,
            )
            copy.start()
            copies[lane] = copy
            pending.append(copy)
        return copies

    def own_products(vector, width, target):
        def rows(step, carry):
            for part_row in range(ROW_STEP):
                row = step * ROW_STEP + part_row
                at = row * SLOTS
                picked = [vector[table_ref[own_at + at + slot]] for slot in range(SLOTS)]
                matrix = weights[pl.ds(at, SLOTS), :, 0:width].reshape(SLOTS * block, width)
                target[row] = jnp.dot(
                    jnp.concatenate(picked, axis=1), matrix, preferred_element_type=jnp.float32
                )
            return carry

        lax.fori_loop(0, dev_rows // ROW_STEP, rows, 0)

    def halo_products(copies, halo, width, target):
        for lane in (1, 2, 0, 3, 4):
            copies[lane].wait_recv()

            def ranks(step, carry):
                for part_rank in range(HMAX // 2):
                    at = lane * HMAX + step * (HMAX // 2) + part_rank
                    matrix = weights[table_ref[entry_at + at], :, 0:width]
                    target[at] = jnp.dot(halo[at], matrix, preferred_element_type=jnp.float32)
                return carry

            lax.fori_loop(0, 2, ranks, 0)

    def all_products(row, target, halo_target):
        summed = target[row]
        for slot in range(1, SLOTS):
            summed = summed + halo_target[table_ref[arrived_at + row * SLOTS + slot]]
        return summed

    node_real = jnp.float32(0.0)
    node_imag = jnp.float32(0.0)
    for index in range(node_count):
        angle = 2.0 * math.pi * (index + 0.5) / node_count
        node_real = jnp.where(node == index, jnp.float32(math.cos(angle)), node_real)
        node_imag = jnp.where(node == index, jnp.float32(math.sin(angle)), node_imag)

    copies = send_halo(0, cols_ref, send_0, halo_0)
    loads[0].wait()
    own_products(cols_ref, block, part_0)
    loads[1].wait()
    halo_products(copies, halo_0, block, prod_0)
    loads[2].wait()
    loads[3].wait()

    def first_rows(step, carry):
        for part_row in range(ROW_STEP):
            row = step * ROW_STEP + part_row
            right = all_products(row, part_0, prod_0)
            rhs[row] = right
            both = jnp.dot(
                right.astype(jnp.bfloat16), inverse[row], preferred_element_type=jnp.float32
            )
            fresh = jnp.concatenate([both[:, 0:block], both[:, block:]], axis=0)
            iterate[row] = fresh
            vec_1[row] = fresh.astype(jnp.bfloat16)
        return carry

    lax.fori_loop(0, dev_rows // ROW_STEP, first_rows, 0)

    chunk = col_count // node_count
    for sweep in range(SWEEPS):
        vector, outgoing, halo = [(vec_1, send_1, halo_1), (vec_2, send_2, halo_2)][sweep]
        copies = send_halo(1 + sweep, vector, outgoing, halo)
        own_products(vector, 2 * block, part)
        halo_products(copies, halo, 2 * block, prod)

        def sweep_rows(step, carry):
            for part_row in range(ROW_STEP):
                row = step * ROW_STEP + part_row
                both = all_products(row, part, prod)
                e_real, a_real = both[:col_count, :block], both[:col_count, block:]
                e_imag, a_imag = both[col_count:, :block], both[col_count:, block:]
                res_real = rhs[row] - (node_real * e_real - node_imag * e_imag - a_real)
                res_imag = -(node_real * e_imag + node_imag * e_real - a_imag)
                residual = jnp.concatenate([res_real, res_imag], axis=0).astype(jnp.bfloat16)
                moved = jnp.dot(residual, inverse[row], preferred_element_type=jnp.float32)
                real = iterate[row, 0:col_count] + (
                    moved[:col_count, :block] - moved[col_count:, block:]
                )
                imag = iterate[row, col_count : 2 * col_count] + (
                    moved[:col_count, block:] + moved[col_count:, :block]
                )
                if sweep < SWEEPS - 1:
                    iterate[row, 0:col_count] = real
                    iterate[row, col_count : 2 * col_count] = imag
                    vec_2[row] = jnp.concatenate([real, imag], axis=0).astype(jnp.bfloat16)
                else:
                    out_real = (node_real * real - node_imag * imag) / node_count
                    out_imag = (node_real * imag + node_imag * real) / node_count
                    for y in range(y_count):
                        for core in range(2):
                            at = (2 * y + core) * chunk
                            share[core, y, row, 0:chunk] = out_real[at : at + chunk]
                            share[core, y, row, chunk : 2 * chunk] = out_imag[at : at + chunk]
            return carry

        lax.fori_loop(0, dev_rows // ROW_STEP, sweep_rows, 0)

    to_core = pltpu.make_async_remote_copy(
        src_ref=share.at[1 - my_core],
        dst_ref=from_core,
        send_sem=core_send,
        recv_sem=core_recv,
        device_id={"node": 2 * my_y + (1 - my_core)},
        device_id_type=MESH,
    )
    to_core.start()
    pending.append(to_core)
    to_core.wait_recv()
    arrivals = []
    for step in range(1, y_count):
        other = lax.rem(my_y + step, y_count)
        mixed[step] = share[my_core, other] + from_core[other]
        copy = pltpu.make_async_remote_copy(
            src_ref=mixed.at[step],
            dst_ref=from_y.at[step - 1],
            send_sem=y_send.at[step - 1],
            recv_sem=y_recv.at[step - 1],
            device_id={"node": 2 * other + my_core},
            device_id_type=MESH,
        )
        copy.start()
        arrivals.append(copy)
        pending.append(copy)
    mixed[0] = share[my_core, my_y] + from_core[my_y]
    for copy in arrivals:
        copy.wait_recv()
    total = mixed[0]
    for step in range(1, y_count):
        total = total + from_y[step - 1]
    out_ref[...] = total
    for copy in pending:
        copy.wait_send()


def per_device(peer_count, node_count, columns, pencil_e, pencil_a, precond, neighbours):
    dev_rows, _, block, _ = pencil_e.shape
    col_count = columns.shape[0]
    pairs = 2 * col_count
    chunk = col_count // node_count
    y_count = node_count // 2
    entries = dev_rows * SLOTS
    table, wanted = index_tables(neighbours, dev_rows, peer_count)
    turned = jnp.pad(columns.transpose(1, 0, 2), ((0, 1), (0, 0), (0, 0)))
    half, full = jnp.bfloat16, jnp.float32
    vmem = pl.BlockSpec(memory_space=pltpu.VMEM)
    anywhere = pl.BlockSpec(memory_space=pl.ANY)
    dma = pltpu.SemaphoreType.DMA
    scratch = [
        pltpu.VMEM((entries, block, 2 * block), half),
        pltpu.VMEM((dev_rows, block, 2 * block), half),
        pltpu.VMEM((LANES, 8, 128), jnp.int32),
        pltpu.SMEM((LANES, 8, 128), jnp.int32),
        pltpu.VMEM((HALO, col_count, block), half),
        pltpu.VMEM((HALO, pairs, block), half),
        pltpu.VMEM((HALO, pairs, block), half),
        pltpu.VMEM((HALO, col_count, block), half),
        pltpu.VMEM((HALO, pairs, block), half),
        pltpu.VMEM((HALO, pairs, block), half),
        pltpu.VMEM((dev_rows + 1, pairs, block), half),
        pltpu.VMEM((dev_rows + 1, pairs, block), half),
        pltpu.VMEM((dev_rows, col_count, block), full),
        pltpu.VMEM((dev_rows, pairs, 2 * block), full),
        pltpu.VMEM((HALO + 1, col_count, block), full),
        pltpu.VMEM((HALO + 1, pairs, 2 * block), full),
        pltpu.VMEM((dev_rows, col_count, block), full),
        pltpu.VMEM((dev_rows, pairs, block), full),
        pltpu.VMEM((2, y_count, dev_rows, 2 * chunk, block), full),
        pltpu.VMEM((y_count, dev_rows, 2 * chunk, block), full),
        pltpu.VMEM((y_count, dev_rows, 2 * chunk, block), full),
        pltpu.VMEM((max(y_count - 1, 1), dev_rows, 2 * chunk, block), full),
        dma((4,)),
        dma,
        dma((LANES,)),
        dma((LANES,)),
        dma((1 + SWEEPS, LANES)),
        dma((1 + SWEEPS, LANES)),
        dma,
        dma,
        dma((max(y_count - 1, 1),)),
        dma((max(y_count - 1, 1),)),
    ]
    summed = pl.pallas_call(
        functools.partial(kernel, peer_count, node_count),
        out_shape=jax.ShapeDtypeStruct((dev_rows, 2 * chunk, block), full),
        in_specs=[
            pl.BlockSpec(memory_space=pltpu.SMEM),
            vmem,
            vmem,
            anywhere,
            anywhere,
            anywhere,
        ],
        out_specs=vmem,
        scratch_shapes=scratch,
        compiler_params=pltpu.CompilerParams(
            collective_id=0, has_side_effects=True, vmem_limit_bytes=60 * 1024 * 1024
        ),
    )(
        table,
        wanted,
        turned,
        pencil_e.reshape(entries, block, block),
        pencil_a.reshape(entries, block, block),
        precond.reshape(2, dev_rows, block, block),
    )
    return summed.reshape(dev_rows, 2, chunk, block).transpose(1, 2, 0, 3)


def solution(mesh):
    placed = (
        P(None, "rows", None),
        P("rows", None, None, None),
        P("rows", None, None, None),
        P("node", None, "rows", None, None),
        P("rows", None),
    )
    return jax.shard_map(
        functools.partial(per_device, mesh.shape["rows"], mesh.shape["node"]),
        mesh=mesh,
        in_specs=placed,
        out_specs=P(None, "node", "rows", None),
        check_vma=False,
    )
```

```python
import functools
import math

import jax
import jax.numpy as jnp
from jax import lax
from jax.experimental import pallas as pl
from jax.experimental.pallas import tpu as pltpu
from jax.sharding import PartitionSpec as P

SLOTS = 5
HMAX = 6
REACH = 2
SWEEPS = 2
LANES = 2 * REACH + 1
HALO = LANES * HMAX
MESH = pl.DeviceIdType.MESH
ROW_STEP = 4


def lane_offsets(peer_count):
    return list(range(-REACH, 0)) + list(range(1, REACH + 1)) + [peer_count // 2]


def index_tables(neighbours, dev_rows, peer_count):
    my_index = lax.axis_index("rows")
    flat = neighbours.reshape(-1)
    owner = flat // dev_rows
    local = flat - owner * dev_rows
    remote = owner != my_index
    half_cycle = peer_count // 2
    off = (owner - my_index + peer_count) % peer_count
    far = off == half_cycle
    off = jnp.where(off > half_cycle, off - peer_count, off)
    lane = jnp.where(off < 0, off + REACH, off + REACH - 1)
    lane = jnp.where(far, 2 * REACH, lane)
    lane = jnp.where(remote, lane, -1)
    position = jnp.arange(flat.shape[0], dtype=jnp.int32)
    earlier = (lane[None, :] == lane[:, None]) & (position[None, :] < position[:, None])
    rank = jnp.sum(earlier.astype(jnp.int32), axis=1)
    place = jnp.where(remote, lane * HMAX + rank, -1)
    matched = place[None, :] == jnp.arange(HALO, dtype=jnp.int32)[:, None]
    entry = jnp.sum(jnp.where(matched, position[None, :], 0), axis=1)
    wanted = jnp.sum(jnp.where(matched, local[None, :], 0), axis=1)
    own = jnp.where(remote, dev_rows, local)
    arrived = jnp.where(remote, place, HALO)
    return own, arrived, entry, wanted.reshape(LANES, 1, HMAX)


def kernel(
    peer_count,
    node_count,
    own_ref,
    arrived_ref,
    entry_ref,
    want_ref,
    cols_ref,
    e_ref,
    a_ref,
    p_ref,
    out_ref,
    weights,
    inverse,
    wide_cols,
    asked_v,
    asked_s,
    vec_0,
    send_0,
    halo_0,
    part_0,
    prod_0,
    rhs,
    vec,
    outgoing,
    halo,
    part,
    prod,
    iterate,
    share,
    from_core,
    mixed,
    to_y,
    from_y,
    load_sem,
    asked_sem,
    want_send,
    want_recv,
    halo_send,
    halo_recv,
    core_send,
    core_recv,
    y_send,
    y_recv,
):
    dev_rows = rhs.shape[0]
    block = rhs.shape[2]
    batches = vec.shape[1]
    width = vec.shape[3] // 2
    chunk = width // 2
    offsets = lane_offsets(peer_count)
    me = lax.axis_index("rows")
    node = lax.axis_index("node")
    my_y = node // 2
    my_core = node % 2

    def batch_y(batch):
        return lax.rem(my_y + 1 + batch, batches)

    load_e = pltpu.make_async_copy(e_ref, weights.at[:, :, 0:block], load_sem.at[0])
    load_a = pltpu.make_async_copy(a_ref, weights.at[:, :, block : 2 * block], load_sem.at[1])
    load_p = [
        pltpu.make_async_copy(
            p_ref.at[index], inverse.at[:, :, index * block : (index + 1) * block], load_sem.at[2 + index]
        )
        for index in range(2)
    ]
    for copy in [load_e] + load_p + [load_a]:
        copy.start()

    def behind(offset):
        return lax.rem(me + offset + peer_count, peer_count)

    barrier = pltpu.get_barrier_semaphore()
    for offset in offsets:
        pl.semaphore_signal(barrier, inc=1, device_id={"rows": behind(offset)}, device_id_type=MESH)
    for step in range(1, node_count):
        other = lax.rem(node + step, node_count)
        pl.semaphore_signal(barrier, inc=1, device_id={"node": other}, device_id_type=MESH)

    wide_cols[...] = cols_ref[...].astype(jnp.float32)
    for row in range(dev_rows):
        for batch in range(batches):
            at = pl.multiple_of(batch_y(batch) * width, width)
            vec_0[row, batch * width : (batch + 1) * width] = wide_cols[pl.ds(at, width), row, :].astype(
                jnp.bfloat16
            )
    vec_0[dev_rows] = jnp.zeros(vec_0.shape[1:], vec_0.dtype)
    prod_0[HALO] = jnp.zeros(prod_0.shape[1:], prod_0.dtype)
    for batch in range(batches):
        prod[batch, HALO] = jnp.zeros(prod.shape[2:], prod.dtype)
        for sweep in range(SWEEPS):
            vec[sweep, batch, dev_rows] = jnp.zeros(vec.shape[3:], vec.dtype)

    pl.semaphore_wait(barrier, LANES + node_count - 1)

    pending = []
    for lane, offset in enumerate(offsets):
        copy = pltpu.make_async_remote_copy(
            src_ref=want_ref.at[lane],
            dst_ref=asked_v.at[lane],
            send_sem=want_send.at[lane],
            recv_sem=want_recv.at[lane],
            device_id={"rows": behind(offset)},
            device_id_type=MESH,
        )
        copy.start()
        pending.append(copy)
    for copy in pending:
        copy.wait_recv()
    to_scalars = pltpu.make_async_copy(asked_v, asked_s, asked_sem)
    to_scalars.start()
    to_scalars.wait()

    def send_halo(phase, source, leaving, arriving):
        copies = [None] * LANES
        for lane in (4, 0, 3, 1, 2):
            for rank in range(HMAX):
                leaving[lane * HMAX + rank] = source[asked_s[lane, 0, rank]]
            here = pl.ds(lane * HMAX, HMAX)
            copy = pltpu.make_async_remote_copy(
                src_ref=leaving.at[here],
                dst_ref=arriving.at[here],
                send_sem=halo_send.at[phase, lane],
                recv_sem=halo_recv.at[phase, lane],
                device_id={"rows": behind(-offsets[lane])},
                device_id_type=MESH,
            )
            copy.start()
            copies[lane] = copy
            pending.append(copy)
        return copies

    def row_loop(body):
        def step_rows(step, carry):
            for inner in range(ROW_STEP):
                body(step * ROW_STEP + inner)
            return carry

        lax.fori_loop(0, dev_rows // ROW_STEP, step_rows, 0)

    def own_products(source, columns, target):
        def one_row(row):
            at = row * SLOTS
            picked = [source[own_ref[at + slot]] for slot in range(SLOTS)]
            matrix = weights[pl.ds(at, SLOTS), :, 0:columns].reshape(SLOTS * block, columns)
            target[row] = jnp.dot(
                jnp.concatenate(picked, axis=1), matrix, preferred_element_type=jnp.float32
            )

        row_loop(one_row)

    def halo_products(copies, arriving, columns, target):
        for lane in (1, 2, 0, 3, 4):
            copies[lane].wait_recv()

            def some_ranks(step, carry):
                for inner in range(HMAX // 2):
                    at = lane * HMAX + step * (HMAX // 2) + inner
                    matrix = weights[entry_ref[at], :, 0:columns]
                    target[at] = jnp.dot(arriving[at], matrix, preferred_element_type=jnp.float32)
                return carry

            lax.fori_loop(0, 2, some_ranks, 0)

    def all_products(row, target, halo_target):
        summed = target[row]
        for slot in range(1, SLOTS):
            summed = summed + halo_target[arrived_ref[row * SLOTS + slot]]
        return summed

    node_real = jnp.float32(0.0)
    node_imag = jnp.float32(0.0)
    for index in range(node_count):
        angle = 2.0 * math.pi * (index + 0.5) / node_count
        node_real = jnp.where(node == index, jnp.float32(math.cos(angle)), node_real)
        node_imag = jnp.where(node == index, jnp.float32(math.sin(angle)), node_imag)

    copies = send_halo(0, vec_0, send_0, halo_0)
    load_e.wait()
    own_products(vec_0, block, part_0)
    load_a.wait()
    halo_products(copies, halo_0, block, prod_0)
    for copy in load_p:
        copy.wait()

    def right_rows(row):
        rhs[row] = all_products(row, part_0, prod_0)

    row_loop(right_rows)

    def phase_of(sweep, batch):
        return 1 + sweep * batches + batch

    flights = {}
    for batch in range(batches):

        def first_rows(row, batch=batch):
            right = rhs[row, batch * width : (batch + 1) * width]
            both = jnp.dot(
                right.astype(jnp.bfloat16), inverse[row], preferred_element_type=jnp.float32
            )
            fresh = jnp.concatenate([both[:, 0:block], both[:, block:]], axis=0)
            iterate[batch, row] = fresh
            vec[0, batch, row] = fresh.astype(jnp.bfloat16)

        row_loop(first_rows)
        flights[0, batch] = send_halo(
            phase_of(0, batch), vec.at[0, batch], outgoing.at[0, batch], halo.at[0, batch]
        )

    core_copies = []
    y_copies = []

    def finish_core(batch):
        core_copies[batch].wait_recv()
        mixed[batch] = share[batch, my_core] + from_core[batch]
        if batch < batches - 1:
            to_y[batch] = mixed[batch].astype(to_y.dtype)
            copy = pltpu.make_async_remote_copy(
                src_ref=to_y.at[batch],
                dst_ref=from_y.at[batch],
                send_sem=y_send.at[batch],
                recv_sem=y_recv.at[batch],
                device_id={"node": 2 * batch_y(batch) + my_core},
                device_id_type=MESH,
            )
            copy.start()
            y_copies.append(copy)
            pending.append(copy)

    for sweep in range(SWEEPS):
        for batch in range(batches):
            source, arriving = vec.at[sweep, batch], halo.at[sweep, batch]
            target, halo_target = part.at[batch], prod.at[batch]
            own_products(source, 2 * block, target)
            if sweep == SWEEPS - 1 and batch > 0:
                finish_core(batch - 1)
            halo_products(flights[sweep, batch], arriving, 2 * block, halo_target)

            def sweep_rows(row, sweep=sweep, batch=batch, target=target, halo_target=halo_target):
                both = all_products(row, target, halo_target)
                e_real, a_real = both[:width, :block], both[:width, block:]
                e_imag, a_imag = both[width:, :block], both[width:, block:]
                right = rhs[row, batch * width : (batch + 1) * width]
                res_real = right - (node_real * e_real - node_imag * e_imag - a_real)
                res_imag = -(node_real * e_imag + node_imag * e_real - a_imag)
                residual = jnp.concatenate([res_real, res_imag], axis=0).astype(jnp.bfloat16)
                moved = jnp.dot(residual, inverse[row], preferred_element_type=jnp.float32)
                real = iterate[batch, row, 0:width] + (
                    moved[:width, :block] - moved[width:, block:]
                )
                imag = iterate[batch, row, width : 2 * width] + (
                    moved[:width, block:] + moved[width:, :block]
                )
                if sweep < SWEEPS - 1:
                    iterate[batch, row, 0:width] = real
                    iterate[batch, row, width : 2 * width] = imag
                    vec[sweep + 1, batch, row] = jnp.concatenate([real, imag], axis=0).astype(
                        jnp.bfloat16
                    )
                else:
                    out_real = (node_real * real - node_imag * imag) / node_count
                    out_imag = (node_real * imag + node_imag * real) / node_count
                    for core in range(2):
                        at = core * chunk
                        share[batch, core, row, 0:chunk] = out_real[at : at + chunk]
                        share[batch, core, row, chunk : 2 * chunk] = out_imag[at : at + chunk]

            row_loop(sweep_rows)
            if sweep < SWEEPS - 1:
                flights[sweep + 1, batch] = send_halo(
                    phase_of(sweep + 1, batch),
                    vec.at[sweep + 1, batch],
                    outgoing.at[sweep + 1, batch],
                    halo.at[sweep + 1, batch],
                )
            else:
                copy = pltpu.make_async_remote_copy(
                    src_ref=share.at[batch, 1 - my_core],
                    dst_ref=from_core.at[batch],
                    send_sem=core_send.at[batch],
                    recv_sem=core_recv.at[batch],
                    device_id={"node": 2 * my_y + (1 - my_core)},
                    device_id_type=MESH,
                )
                copy.start()
                core_copies.append(copy)
                pending.append(copy)

    finish_core(batches - 1)
    for copy in y_copies:
        copy.wait_recv()
    for row in range(dev_rows):
        total = mixed[batches - 1, row]
        for batch in range(batches - 1):
            total = total + from_y[batch, row].astype(jnp.float32)
        out_ref[:, row, :] = total
    for copy in pending:
        copy.wait_send()


def per_device(peer_count, node_count, columns, pencil_e, pencil_a, precond, neighbours):
    dev_rows, _, block, _ = pencil_e.shape
    col_count = columns.shape[0]
    batches = node_count // 2
    width = col_count // batches
    chunk = width // 2
    entries = dev_rows * SLOTS
    tables = index_tables(neighbours, dev_rows, peer_count)
    half, full = jnp.bfloat16, jnp.float32
    smem = pl.BlockSpec(memory_space=pltpu.SMEM)
    vmem = pl.BlockSpec(memory_space=pltpu.VMEM)
    anywhere = pl.BlockSpec(memory_space=pl.ANY)
    dma = pltpu.SemaphoreType.DMA
    crossings = max(batches - 1, 1)
    scratch = [
        pltpu.VMEM((entries, block, 2 * block), half),
        pltpu.VMEM((dev_rows, block, 2 * block), half),
        pltpu.VMEM((col_count, dev_rows, block), full),
        pltpu.VMEM((LANES, 1, HMAX), jnp.int32),
        pltpu.SMEM((LANES, 1, HMAX), jnp.int32),
        pltpu.VMEM((dev_rows + 1, col_count, block), half),
        pltpu.VMEM((HALO, col_count, block), half),
        pltpu.VMEM((HALO, col_count, block), half),
        pltpu.VMEM((dev_rows, col_count, block), full),
        pltpu.VMEM((HALO + 1, col_count, block), full),
        pltpu.VMEM((dev_rows, col_count, block), full),
        pltpu.VMEM((SWEEPS, batches, dev_rows + 1, 2 * width, block), half),
        pltpu.VMEM((SWEEPS, batches, HALO, 2 * width, block), half),
        pltpu.VMEM((SWEEPS, batches, HALO, 2 * width, block), half),
        pltpu.VMEM((batches, dev_rows, 2 * width, 2 * block), full),
        pltpu.VMEM((batches, HALO + 1, 2 * width, 2 * block), full),
        pltpu.VMEM((batches, dev_rows, 2 * width, block), full),
        pltpu.VMEM((batches, 2, dev_rows, 2 * chunk, block), full),
        pltpu.VMEM((batches, dev_rows, 2 * chunk, block), full),
        pltpu.VMEM((batches, dev_rows, 2 * chunk, block), full),
        pltpu.VMEM((crossings, dev_rows, 2 * chunk, block), half),
        pltpu.VMEM((crossings, dev_rows, 2 * chunk, block), half),
        dma((4,)),
        dma,
        dma((LANES,)),
        dma((LANES,)),
        dma((1 + SWEEPS * batches, LANES)),
        dma((1 + SWEEPS * batches, LANES)),
        dma((batches,)),
        dma((batches,)),
        dma((crossings,)),
        dma((crossings,)),
    ]
    summed = pl.pallas_call(
        functools.partial(kernel, peer_count, node_count),
        out_shape=jax.ShapeDtypeStruct((2 * chunk, dev_rows, block), full),
        in_specs=[smem, smem, smem, vmem, vmem, anywhere, anywhere, anywhere],
        out_specs=vmem,
        scratch_shapes=scratch,
        compiler_params=pltpu.CompilerParams(
            collective_id=0, has_side_effects=True, vmem_limit_bytes=60 * 1024 * 1024
        ),
    )(
        *tables,
        columns,
        pencil_e.reshape(entries, block, block),
        pencil_a.reshape(entries, block, block),
        precond.reshape(2, dev_rows, block, block),
    )
    return summed.reshape(2, chunk, dev_rows, block)


def solution(mesh):
    placed = (
        P(None, "rows", None),
        P("rows", None, None, None),
        P("rows", None, None, None),
        P("node", None, "rows", None, None),
        P("rows", None),
    )
    return jax.shard_map(
        functools.partial(per_device, mesh.shape["rows"], mesh.shape["node"]),
        mesh=mesh,
        in_specs=placed,
        out_specs=P(None, "node", "rows", None),
        check_vma=False,
    )
```

```python
import functools
import math

import jax
import jax.numpy as jnp
from jax import lax
from jax.experimental import pallas as pl
from jax.experimental.pallas import tpu as pltpu
from jax.sharding import PartitionSpec as P

SLOTS = 5
HMAX = 6
REACH = 2
SWEEPS = 2
LANES = 2 * REACH + 1
HALO = LANES * HMAX
MESH = pl.DeviceIdType.MESH
ROW_STEP = 8


def lane_offsets(peer_count):
    return list(range(-REACH, 0)) + list(range(1, REACH + 1)) + [peer_count // 2]


def lane_sum(value):
    shift = value.shape[1] // 2
    while shift:
        value = value + pltpu.roll(value, shift, 1)
        shift //= 2
    return value


def index_tables(neighbours, dev_rows, me, owners):
    wide = 128
    entries = dev_rows * SLOTS
    position = lax.broadcasted_iota(jnp.int32, (8, wide), 1)
    sub = lax.broadcasted_iota(jnp.int32, (8, wide), 0)
    flat = jnp.zeros((8, wide), jnp.int32)
    slot_of = jnp.zeros((8, wide), jnp.int32)
    for slot in range(SLOTS):
        line = jnp.broadcast_to(neighbours[slot : slot + 1, :], (8, wide))
        flat = flat + (pltpu.roll(line, slot * dev_rows, 1) if slot else line)
        if slot:
            slot_of = slot_of + (position >= slot * dev_rows).astype(jnp.int32)
    row_of = position - slot_of * dev_rows
    first = jnp.zeros((8, wide), jnp.int32)
    for lane, owner in enumerate(owners):
        first = jnp.where(sub == lane, owner * dev_rows, first)
    inside = (flat >= first) & (flat < first + dev_rows) & (sub < LANES) & (position < entries)
    count = jnp.where(inside, 1, 0)
    shift = 1
    while shift < wide:
        count = count + jnp.where(position >= shift, pltpu.roll(count, shift, 1), 0)
        shift *= 2
    rank = count - 1

    def over_lanes(value):
        value = jnp.where(inside, value, 0)
        for step in (4, 2, 1):
            value = value + pltpu.roll(value, step, 0)
        return value

    remote = over_lanes(jnp.ones_like(flat)) > 0
    arrived = jnp.clip(jnp.where(remote, over_lanes(sub * HMAX + rank), HALO), 0, HALO)
    place = jnp.where(remote, over_lanes(sub * 8 + rank), -1)
    local = flat - over_lanes(first)
    own = jnp.clip(jnp.where(remote, dev_rows, flat - me * dev_rows), 0, dev_rows)
    entry_of = row_of * SLOTS + slot_of
    entry, wanted = [], []
    for lane in range(LANES):
        matched = place == sub + lane * 8
        entry.append(jnp.clip(lane_sum(jnp.where(matched, entry_of, 0)), 0, entries - 1))
        wanted.append(jnp.clip(lane_sum(jnp.where(matched, local, 0)), 0, dev_rows - 1))
    return own, arrived, entry, wanted


def kernel(
    peer_count,
    node_count,
    near_ref,
    cols_ref,
    e_ref,
    a_ref,
    p_ref,
    out_ref,
    weights,
    inverse,
    wide_cols,
    near,
    table_v,
    table_s,
    want_v,
    asked_v,
    asked_s,
    vec_0,
    send_0,
    halo_0,
    part_0,
    prod_0,
    rhs,
    vec,
    outgoing,
    halo,
    part,
    prod,
    iterate,
    share,
    from_core,
    mixed,
    from_y,
    load_sem,
    table_sem,
    asked_sem,
    want_send,
    want_recv,
    halo_send,
    halo_recv,
    core_send,
    core_recv,
    y_send,
    y_recv,
):
    dev_rows = rhs.shape[0]
    block = rhs.shape[2]
    batches = vec.shape[1]
    width = vec.shape[3] // 2
    chunk = width // 2
    offsets = lane_offsets(peer_count)
    me = lax.axis_index("rows")
    node = lax.axis_index("node")
    my_y = node // 2
    my_core = node % 2

    def batch_y(batch):
        return lax.rem(my_y + 1 + batch, batches)

    load_e = pltpu.make_async_copy(e_ref, weights.at[:, :, 0:block], load_sem.at[0])
    load_a = pltpu.make_async_copy(a_ref, weights.at[:, :, block : 2 * block], load_sem.at[1])
    load_p = [
        pltpu.make_async_copy(
            p_ref.at[index], inverse.at[:, :, index * block : (index + 1) * block], load_sem.at[2 + index]
        )
        for index in range(2)
    ]
    for copy in [load_e] + load_p + [load_a]:
        copy.start()

    def behind(offset):
        return lax.rem(me + offset + peer_count, peer_count)

    barrier = pltpu.get_barrier_semaphore()
    for offset in offsets:
        pl.semaphore_signal(barrier, inc=1, device_id={"rows": behind(offset)}, device_id_type=MESH)
    for step in range(1, node_count):
        other = lax.rem(node + step, node_count)
        pl.semaphore_signal(barrier, inc=1, device_id={"node": other}, device_id_type=MESH)

    near[...] = jnp.zeros(near.shape, near.dtype)
    near[0:SLOTS, 0:dev_rows] = near_ref[...]
    own, arrived, entry, wanted = index_tables(
        near[...], dev_rows, me, [behind(offset) for offset in offsets]
    )
    for lane in range(LANES):
        want_v[lane] = wanted[lane]
        table_v[lane] = entry[lane]
    table_v[LANES] = own
    table_v[LANES + 1] = arrived
    to_table = pltpu.make_async_copy(table_v, table_s, table_sem)
    to_table.start()

    wide_cols[...] = cols_ref[...].astype(jnp.float32)
    for row in range(dev_rows):
        for batch in range(batches):
            at = pl.multiple_of(batch_y(batch) * width, width)
            vec_0[row, batch * width : (batch + 1) * width] = wide_cols[pl.ds(at, width), row, :].astype(
                jnp.bfloat16
            )
    vec_0[dev_rows] = jnp.zeros(vec_0.shape[1:], vec_0.dtype)
    prod_0[HALO] = jnp.zeros(prod_0.shape[1:], prod_0.dtype)
    for batch in range(batches):
        prod[batch, HALO] = jnp.zeros(prod.shape[2:], prod.dtype)
        for sweep in range(SWEEPS):
            vec[sweep, batch, dev_rows] = jnp.zeros(vec.shape[3:], vec.dtype)

    pl.semaphore_wait(barrier, LANES + node_count - 1)

    pending = []
    for lane, offset in enumerate(offsets):
        copy = pltpu.make_async_remote_copy(
            src_ref=want_v.at[lane],
            dst_ref=asked_v.at[lane],
            send_sem=want_send.at[lane],
            recv_sem=want_recv.at[lane],
            device_id={"rows": behind(offset)},
            device_id_type=MESH,
        )
        copy.start()
        pending.append(copy)
    for copy in pending:
        copy.wait_recv()
    to_scalars = pltpu.make_async_copy(asked_v, asked_s, asked_sem)
    to_scalars.start()
    to_scalars.wait()
    to_table.wait()

    def send_halo(phase, source, leaving, arriving):
        copies = [None] * LANES
        for lane in (4, 0, 3, 1, 2):
            for rank in range(HMAX):
                leaving[lane * HMAX + rank] = source[asked_s[lane, rank, 0]]
            here = pl.ds(lane * HMAX, HMAX)
            copy = pltpu.make_async_remote_copy(
                src_ref=leaving.at[here],
                dst_ref=arriving.at[here],
                send_sem=halo_send.at[phase, lane],
                recv_sem=halo_recv.at[phase, lane],
                device_id={"rows": behind(-offsets[lane])},
                device_id_type=MESH,
            )
            copy.start()
            copies[lane] = copy
            pending.append(copy)
        return copies

    def row_loop(body):
        def step_rows(step, carry):
            for inner in range(ROW_STEP):
                body(step * ROW_STEP + inner)
            return carry

        lax.fori_loop(0, dev_rows // ROW_STEP, step_rows, 0)

    def own_products(source, columns, target):
        def one_row(row):
            at = row * SLOTS
            picked = [source[table_s[LANES, 0, slot * dev_rows + row]] for slot in range(SLOTS)]
            matrix = weights[pl.ds(at, SLOTS), :, 0:columns].reshape(SLOTS * block, columns)
            target[row] = jnp.dot(
                jnp.concatenate(picked, axis=1), matrix, preferred_element_type=jnp.float32
            )

        row_loop(one_row)

    def halo_products(copies, arriving, columns, target):
        for lane in (1, 2, 0, 3, 4):
            copies[lane].wait_recv()

            for rank in range(HMAX):
                at = lane * HMAX + rank
                matrix = weights[table_s[lane, rank, 0], :, 0:columns]
                target[at] = jnp.dot(arriving[at], matrix, preferred_element_type=jnp.float32)

    def all_products(row, target, halo_target):
        summed = target[row]
        for slot in range(1, SLOTS):
            summed = summed + halo_target[table_s[LANES + 1, 0, slot * dev_rows + row]]
        return summed

    node_real = jnp.float32(0.0)
    node_imag = jnp.float32(0.0)
    for index in range(node_count):
        angle = 2.0 * math.pi * (index + 0.5) / node_count
        node_real = jnp.where(node == index, jnp.float32(math.cos(angle)), node_real)
        node_imag = jnp.where(node == index, jnp.float32(math.sin(angle)), node_imag)

    copies = send_halo(0, vec_0, send_0, halo_0)
    load_e.wait()
    own_products(vec_0, block, part_0)
    load_a.wait()
    halo_products(copies, halo_0, block, prod_0)
    for copy in load_p:
        copy.wait()

    def right_rows(row):
        rhs[row] = all_products(row, part_0, prod_0)

    row_loop(right_rows)

    def phase_of(sweep, batch):
        return 1 + sweep * batches + batch

    flights = {}
    for batch in range(batches):

        def first_rows(row, batch=batch):
            right = rhs[row, batch * width : (batch + 1) * width]
            both = jnp.dot(
                right.astype(jnp.bfloat16), inverse[row], preferred_element_type=jnp.float32
            )
            fresh = jnp.concatenate([both[:, 0:block], both[:, block:]], axis=0)
            iterate[batch, row] = fresh
            vec[0, batch, row] = fresh.astype(jnp.bfloat16)

        row_loop(first_rows)
        flights[0, batch] = send_halo(
            phase_of(0, batch), vec.at[0, batch], outgoing.at[0, batch], halo.at[0, batch]
        )

    core_copies = []
    y_copies = []

    def finish_core(batch):
        core_copies[batch].wait_recv()
        mixed[batch] = share[batch, my_core] + from_core[batch]
        if batch < batches - 1:
            copy = pltpu.make_async_remote_copy(
                src_ref=mixed.at[batch],
                dst_ref=from_y.at[batch],
                send_sem=y_send.at[batch],
                recv_sem=y_recv.at[batch],
                device_id={"node": 2 * batch_y(batch) + my_core},
                device_id_type=MESH,
            )
            copy.start()
            y_copies.append(copy)
            pending.append(copy)

    for sweep in range(SWEEPS):
        for batch in range(batches):
            source, arriving = vec.at[sweep, batch], halo.at[sweep, batch]
            target, halo_target = part.at[batch], prod.at[batch]
            own_products(source, 2 * block, target)
            if sweep == SWEEPS - 1 and batch > 0:
                finish_core(batch - 1)
            halo_products(flights[sweep, batch], arriving, 2 * block, halo_target)

            def sweep_rows(row, sweep=sweep, batch=batch, target=target, halo_target=halo_target):
                both = all_products(row, target, halo_target)
                e_real, a_real = both[:width, :block], both[:width, block:]
                e_imag, a_imag = both[width:, :block], both[width:, block:]
                right = rhs[row, batch * width : (batch + 1) * width]
                res_real = right - (node_real * e_real - node_imag * e_imag - a_real)
                res_imag = -(node_real * e_imag + node_imag * e_real - a_imag)
                residual = jnp.concatenate([res_real, res_imag], axis=0).astype(jnp.bfloat16)
                moved = jnp.dot(residual, inverse[row], preferred_element_type=jnp.float32)
                real = iterate[batch, row, 0:width] + (
                    moved[:width, :block] - moved[width:, block:]
                )
                imag = iterate[batch, row, width : 2 * width] + (
                    moved[:width, block:] + moved[width:, :block]
                )
                if sweep < SWEEPS - 1:
                    iterate[batch, row, 0:width] = real
                    iterate[batch, row, width : 2 * width] = imag
                    vec[sweep + 1, batch, row] = jnp.concatenate([real, imag], axis=0).astype(
                        jnp.bfloat16
                    )
                else:
                    out_real = node_real * real - node_imag * imag
                    out_imag = node_real * imag + node_imag * real
                    for core in range(2):
                        at = core * chunk
                        share[batch, core, row, 0:chunk] = out_real[at : at + chunk]
                        share[batch, core, row, chunk : 2 * chunk] = out_imag[at : at + chunk]

            row_loop(sweep_rows)
            if sweep < SWEEPS - 1:
                flights[sweep + 1, batch] = send_halo(
                    phase_of(sweep + 1, batch),
                    vec.at[sweep + 1, batch],
                    outgoing.at[sweep + 1, batch],
                    halo.at[sweep + 1, batch],
                )
            else:
                copy = pltpu.make_async_remote_copy(
                    src_ref=share.at[batch, 1 - my_core],
                    dst_ref=from_core.at[batch],
                    send_sem=core_send.at[batch],
                    recv_sem=core_recv.at[batch],
                    device_id={"node": 2 * my_y + (1 - my_core)},
                    device_id_type=MESH,
                )
                copy.start()
                core_copies.append(copy)
                pending.append(copy)

    finish_core(batches - 1)
    for copy in y_copies:
        copy.wait_recv()
    for row in range(dev_rows):
        total = mixed[batches - 1, row]
        for batch in range(batches - 1):
            total = total + from_y[batch, row]
        out_ref[:, row, :] = total
    for copy in pending:
        copy.wait_send()


def per_device(peer_count, node_count, columns, pencil_e, pencil_a, precond, neighbours):
    dev_rows, _, block, _ = pencil_e.shape
    col_count = columns.shape[0]
    batches = node_count // 2
    width = col_count // batches
    chunk = width // 2
    entries = dev_rows * SLOTS
    half, full = jnp.bfloat16, jnp.float32
    vmem = pl.BlockSpec(memory_space=pltpu.VMEM)
    anywhere = pl.BlockSpec(memory_space=pl.ANY)
    dma = pltpu.SemaphoreType.DMA
    crossings = max(batches - 1, 1)
    scratch = [
        pltpu.VMEM((entries, block, 2 * block), half),
        pltpu.VMEM((dev_rows, block, 2 * block), half),
        pltpu.VMEM((col_count, dev_rows, block), full),
        pltpu.VMEM((8, 128), jnp.int32),
        pltpu.VMEM((LANES + 2, 8, 128), jnp.int32),
        pltpu.SMEM((LANES + 2, 8, 128), jnp.int32),
        pltpu.VMEM((LANES, 8, 128), jnp.int32),
        pltpu.VMEM((LANES, 8, 128), jnp.int32),
        pltpu.SMEM((LANES, 8, 128), jnp.int32),
        pltpu.VMEM((dev_rows + 1, col_count, block), half),
        pltpu.VMEM((HALO, col_count, block), half),
        pltpu.VMEM((HALO, col_count, block), half),
        pltpu.VMEM((dev_rows, col_count, block), full),
        pltpu.VMEM((HALO + 1, col_count, block), full),
        pltpu.VMEM((dev_rows, col_count, block), full),
        pltpu.VMEM((SWEEPS, batches, dev_rows + 1, 2 * width, block), half),
        pltpu.VMEM((SWEEPS, batches, HALO, 2 * width, block), half),
        pltpu.VMEM((SWEEPS, batches, HALO, 2 * width, block), half),
        pltpu.VMEM((batches, dev_rows, 2 * width, 2 * block), full),
        pltpu.VMEM((batches, HALO + 1, 2 * width, 2 * block), full),
        pltpu.VMEM((batches, dev_rows, 2 * width, block), full),
        pltpu.VMEM((batches, 2, dev_rows, 2 * chunk, block), full),
        pltpu.VMEM((batches, dev_rows, 2 * chunk, block), full),
        pltpu.VMEM((batches, dev_rows, 2 * chunk, block), full),
        pltpu.VMEM((crossings, dev_rows, 2 * chunk, block), full),
        dma((4,)),
        dma,
        dma,
        dma((LANES,)),
        dma((LANES,)),
        dma((1 + SWEEPS * batches, LANES)),
        dma((1 + SWEEPS * batches, LANES)),
        dma((batches,)),
        dma((batches,)),
        dma((crossings,)),
        dma((crossings,)),
    ]
    summed = pl.pallas_call(
        functools.partial(kernel, peer_count, node_count),
        out_shape=jax.ShapeDtypeStruct((2 * chunk, dev_rows, block), full),
        in_specs=[vmem, vmem, anywhere, anywhere, anywhere],
        out_specs=vmem,
        scratch_shapes=scratch,
        compiler_params=pltpu.CompilerParams(
            collective_id=0, has_side_effects=True, vmem_limit_bytes=60 * 1024 * 1024
        ),
    )(
        neighbours.T,
        columns,
        pencil_e.reshape(entries, block, block),
        pencil_a.reshape(entries, block, block),
        precond.reshape(2, dev_rows, block, block),
    )
    return summed.reshape(2, chunk, dev_rows, block) * (1.0 / node_count)


def solution(mesh):
    placed = (
        P(None, "rows", None),
        P("rows", None, None, None),
        P("rows", None, None, None),
        P("node", None, "rows", None, None),
        P("rows", None),
    )
    return jax.shard_map(
        functools.partial(per_device, mesh.shape["rows"], mesh.shape["node"]),
        mesh=mesh,
        in_specs=placed,
        out_specs=P(None, "node", "rows", None),
        check_vma=False,
    )
```

```python
import functools
import math

import jax
import jax.numpy as jnp
from jax import lax
from jax.experimental import pallas as pl
from jax.experimental.pallas import tpu as pltpu
from jax.sharding import PartitionSpec as P

SLOTS = 5
HMAX = 6
REACH = 2
SWEEPS = 2
LANES = 2 * REACH + 1
HALO = LANES * HMAX
MESH = pl.DeviceIdType.MESH
ROW_STEP = 8


def lane_offsets(peer_count):
    return list(range(-REACH, 0)) + list(range(1, REACH + 1)) + [peer_count // 2]


def lane_sum(value):
    shift = value.shape[1] // 2
    while shift:
        value = value + pltpu.roll(value, shift, 1)
        shift //= 2
    return value


def index_tables(neighbours, dev_rows, me, owners):
    wide = 128
    entries = dev_rows * SLOTS
    position = lax.broadcasted_iota(jnp.int32, (8, wide), 1)
    sub = lax.broadcasted_iota(jnp.int32, (8, wide), 0)
    flat = jnp.zeros((8, wide), jnp.int32)
    slot_of = jnp.zeros((8, wide), jnp.int32)
    for slot in range(SLOTS):
        line = jnp.broadcast_to(neighbours[slot : slot + 1, :], (8, wide))
        flat = flat + (pltpu.roll(line, slot * dev_rows, 1) if slot else line)
        if slot:
            slot_of = slot_of + (position >= slot * dev_rows).astype(jnp.int32)
    row_of = position - slot_of * dev_rows
    first = jnp.zeros((8, wide), jnp.int32)
    for lane, owner in enumerate(owners):
        first = jnp.where(sub == lane, owner * dev_rows, first)
    inside = (flat >= first) & (flat < first + dev_rows) & (sub < LANES) & (position < entries)
    count = jnp.where(inside, 1, 0)
    shift = 1
    while shift < wide:
        count = count + jnp.where(position >= shift, pltpu.roll(count, shift, 1), 0)
        shift *= 2
    rank = count - 1

    def over_lanes(value):
        value = jnp.where(inside, value, 0)
        for step in (4, 2, 1):
            value = value + pltpu.roll(value, step, 0)
        return value

    remote = over_lanes(jnp.ones_like(flat)) > 0
    arrived = jnp.clip(jnp.where(remote, over_lanes(sub * HMAX + rank), HALO), 0, HALO)
    place = jnp.where(remote, over_lanes(sub * 8 + rank), -1)
    local = flat - over_lanes(first)
    own = jnp.clip(jnp.where(remote, dev_rows, flat - me * dev_rows), 0, dev_rows)
    entry_of = row_of * SLOTS + slot_of
    entry, wanted = [], []
    for lane in range(LANES):
        matched = place == sub + lane * 8
        entry.append(jnp.clip(lane_sum(jnp.where(matched, entry_of, 0)), 0, entries - 1))
        wanted.append(jnp.clip(lane_sum(jnp.where(matched, local, 0)), 0, dev_rows - 1))
    return own, arrived, entry, wanted


def kernel(
    peer_count,
    node_count,
    near_ref,
    cols_ref,
    e_ref,
    a_ref,
    p_ref,
    out_ref,
    weights,
    inverse,
    wide_cols,
    near,
    table_v,
    table_s,
    want_v,
    asked_v,
    asked_s,
    vec_0,
    send_0,
    halo_0,
    part_0,
    prod_0,
    rhs,
    vec,
    outgoing,
    halo,
    part,
    prod,
    iterate,
    share,
    from_core,
    mixed,
    from_y,
    load_sem,
    table_sem,
    asked_sem,
    want_send,
    want_recv,
    halo_send,
    halo_recv,
    core_send,
    core_recv,
    y_send,
    y_recv,
):
    batches, dev_rows, width, block = rhs.shape
    chunk = width // 2
    offsets = lane_offsets(peer_count)
    me = lax.axis_index("rows")
    node = lax.axis_index("node")
    my_y = node // 2
    my_core = node % 2

    def batch_y(batch):
        return lax.rem(my_y + 1 + batch, batches)

    load_e = pltpu.make_async_copy(e_ref, weights.at[:, :, 0:block], load_sem.at[0])
    load_a = pltpu.make_async_copy(a_ref, weights.at[:, :, block : 2 * block], load_sem.at[1])
    load_p = [
        pltpu.make_async_copy(
            p_ref.at[index], inverse.at[:, :, index * block : (index + 1) * block], load_sem.at[2 + index]
        )
        for index in range(2)
    ]
    for copy in [load_e] + load_p + [load_a]:
        copy.start()

    def behind(offset):
        return lax.rem(me + offset + peer_count, peer_count)

    barrier = pltpu.get_barrier_semaphore()
    for offset in offsets:
        pl.semaphore_signal(barrier, inc=1, device_id={"rows": behind(offset)}, device_id_type=MESH)
    for step in range(1, node_count):
        other = lax.rem(node + step, node_count)
        pl.semaphore_signal(barrier, inc=1, device_id={"node": other}, device_id_type=MESH)

    near[...] = jnp.zeros(near.shape, near.dtype)
    near[0:SLOTS, 0:dev_rows] = near_ref[...]
    own, arrived, entry, wanted = index_tables(
        near[...], dev_rows, me, [behind(offset) for offset in offsets]
    )
    for lane in range(LANES):
        want_v[lane] = wanted[lane]
        table_v[lane] = entry[lane]
    table_v[LANES] = own
    table_v[LANES + 1] = arrived
    to_table = pltpu.make_async_copy(table_v, table_s, table_sem)
    to_table.start()

    wide_cols[...] = cols_ref[...].astype(jnp.float32)
    for row in range(dev_rows):
        for batch in range(batches):
            at = pl.multiple_of(batch_y(batch) * width, width)
            vec_0[row, batch * width : (batch + 1) * width] = wide_cols[pl.ds(at, width), row, :].astype(
                jnp.bfloat16
            )
    vec_0[dev_rows] = jnp.zeros(vec_0.shape[1:], vec_0.dtype)
    for batch in range(batches):
        prod_0[batch, HALO] = jnp.zeros(prod_0.shape[2:], prod_0.dtype)
        prod[batch, HALO] = jnp.zeros(prod.shape[2:], prod.dtype)
    for sweep in range(SWEEPS):
        vec[sweep, dev_rows] = jnp.zeros(vec.shape[2:], vec.dtype)

    pl.semaphore_wait(barrier, LANES + node_count - 1)

    pending = []
    for lane, offset in enumerate(offsets):
        copy = pltpu.make_async_remote_copy(
            src_ref=want_v.at[lane],
            dst_ref=asked_v.at[lane],
            send_sem=want_send.at[lane],
            recv_sem=want_recv.at[lane],
            device_id={"rows": behind(offset)},
            device_id_type=MESH,
        )
        copy.start()
        pending.append(copy)
    for copy in pending:
        copy.wait_recv()
    to_scalars = pltpu.make_async_copy(asked_v, asked_s, asked_sem)
    to_scalars.start()
    to_scalars.wait()
    to_table.wait()

    def send_halo(phase, source, batch, rows, leaving, arriving):
        copies = [None] * LANES
        for lane in (4, 0, 3, 1, 2):
            for rank in range(HMAX):
                leaving[lane * HMAX + rank] = source[
                    asked_s[lane, rank, 0], batch * rows : (batch + 1) * rows
                ]
            here = pl.ds(lane * HMAX, HMAX)
            copy = pltpu.make_async_remote_copy(
                src_ref=leaving.at[here],
                dst_ref=arriving.at[here],
                send_sem=halo_send.at[phase, lane],
                recv_sem=halo_recv.at[phase, lane],
                device_id={"rows": behind(-offsets[lane])},
                device_id_type=MESH,
            )
            copy.start()
            copies[lane] = copy
            pending.append(copy)
        return copies

    def row_loop(body):
        def step_rows(step, carry):
            for inner in range(ROW_STEP):
                body(step * ROW_STEP + inner)
            return carry

        lax.fori_loop(0, dev_rows // ROW_STEP, step_rows, 0)

    def own_products(source, columns, target):
        def one_row(row):
            at = row * SLOTS
            picked = [source[table_s[LANES, 0, slot * dev_rows + row]] for slot in range(SLOTS)]
            matrix = weights[pl.ds(at, SLOTS), :, 0:columns].reshape(SLOTS * block, columns)
            target[row] = jnp.dot(
                jnp.concatenate(picked, axis=1), matrix, preferred_element_type=jnp.float32
            )

        row_loop(one_row)

    def halo_products(copies, arriving, columns, target):
        for lane in (1, 2, 0, 3, 4):
            copies[lane].wait_recv()

            for rank in range(HMAX):
                at = lane * HMAX + rank
                matrix = weights[table_s[lane, rank, 0], :, 0:columns]
                target[at] = jnp.dot(arriving[at], matrix, preferred_element_type=jnp.float32)

    def all_products(row, target, batch, rows, halo_target):
        summed = target[row, batch * rows : (batch + 1) * rows]
        for slot in range(1, SLOTS):
            summed = summed + halo_target[table_s[LANES + 1, 0, slot * dev_rows + row]]
        return summed

    node_real = jnp.float32(0.0)
    node_imag = jnp.float32(0.0)
    for index in range(node_count):
        angle = 2.0 * math.pi * (index + 0.5) / node_count
        node_real = jnp.where(node == index, jnp.float32(math.cos(angle)), node_real)
        node_imag = jnp.where(node == index, jnp.float32(math.sin(angle)), node_imag)

    def phase_of(sweep, batch):
        return (1 + sweep) * batches + batch

    flights = {}
    for batch in range(batches):
        flights[-1, batch] = send_halo(
            phase_of(-1, batch), vec_0, batch, width, send_0.at[batch], halo_0.at[batch]
        )
    load_e.wait()
    own_products(vec_0, block, part_0)
    load_a.wait()
    for copy in load_p:
        copy.wait()

    for batch in range(batches):
        halo_products(flights[-1, batch], halo_0.at[batch], block, prod_0.at[batch])

        def first_rows(row, batch=batch):
            right = all_products(row, part_0, batch, width, prod_0.at[batch])
            rhs[batch, row] = right
            both = jnp.dot(
                right.astype(jnp.bfloat16), inverse[row], preferred_element_type=jnp.float32
            )
            fresh = jnp.concatenate([both[:, 0:block], both[:, block:]], axis=0)
            iterate[batch, row] = fresh
            vec[0, row, batch * 2 * width : (batch + 1) * 2 * width] = fresh.astype(jnp.bfloat16)

        row_loop(first_rows)
        flights[0, batch] = send_halo(
            phase_of(0, batch), vec.at[0], batch, 2 * width, outgoing.at[0, batch], halo.at[0, batch]
        )

    core_copies = []
    y_copies = []

    def finish_core(batch):
        core_copies[batch].wait_recv()
        mixed[batch] = share[batch, my_core] + from_core[batch]
        if batch < batches - 1:
            copy = pltpu.make_async_remote_copy(
                src_ref=mixed.at[batch],
                dst_ref=from_y.at[batch],
                send_sem=y_send.at[batch],
                recv_sem=y_recv.at[batch],
                device_id={"node": 2 * batch_y(batch) + my_core},
                device_id_type=MESH,
            )
            copy.start()
            y_copies.append(copy)
            pending.append(copy)

    for sweep in range(SWEEPS):
        own_products(vec.at[sweep], 2 * block, part)
        for batch in range(batches):
            arriving, halo_target = halo.at[sweep, batch], prod.at[batch]
            if sweep == SWEEPS - 1 and batch > 0:
                finish_core(batch - 1)
            halo_products(flights[sweep, batch], arriving, 2 * block, halo_target)

            def sweep_rows(row, sweep=sweep, batch=batch, halo_target=halo_target):
                both = all_products(row, part, batch, 2 * width, halo_target)
                e_real, a_real = both[:width, :block], both[:width, block:]
                e_imag, a_imag = both[width:, :block], both[width:, block:]
                right = rhs[batch, row]
                res_real = right - (node_real * e_real - node_imag * e_imag - a_real)
                res_imag = -(node_real * e_imag + node_imag * e_real - a_imag)
                residual = jnp.concatenate([res_real, res_imag], axis=0).astype(jnp.bfloat16)
                moved = jnp.dot(residual, inverse[row], preferred_element_type=jnp.float32)
                real = iterate[batch, row, 0:width] + (
                    moved[:width, :block] - moved[width:, block:]
                )
                imag = iterate[batch, row, width : 2 * width] + (
                    moved[:width, block:] + moved[width:, :block]
                )
                if sweep < SWEEPS - 1:
                    iterate[batch, row, 0:width] = real
                    iterate[batch, row, width : 2 * width] = imag
                    vec[sweep + 1, row, batch * 2 * width : (batch + 1) * 2 * width] = (
                        jnp.concatenate([real, imag], axis=0).astype(jnp.bfloat16)
                    )
                else:
                    out_real = node_real * real - node_imag * imag
                    out_imag = node_real * imag + node_imag * real
                    for core in range(2):
                        at = core * chunk
                        share[batch, core, row, 0:chunk] = out_real[at : at + chunk]
                        share[batch, core, row, chunk : 2 * chunk] = out_imag[at : at + chunk]

            row_loop(sweep_rows)
            if sweep < SWEEPS - 1:
                flights[sweep + 1, batch] = send_halo(
                    phase_of(sweep + 1, batch),
                    vec.at[sweep + 1],
                    batch,
                    2 * width,
                    outgoing.at[sweep + 1, batch],
                    halo.at[sweep + 1, batch],
                )
            else:
                copy = pltpu.make_async_remote_copy(
                    src_ref=share.at[batch, 1 - my_core],
                    dst_ref=from_core.at[batch],
                    send_sem=core_send.at[batch],
                    recv_sem=core_recv.at[batch],
                    device_id={"node": 2 * my_y + (1 - my_core)},
                    device_id_type=MESH,
                )
                copy.start()
                core_copies.append(copy)
                pending.append(copy)

    finish_core(batches - 1)
    for copy in y_copies:
        copy.wait_recv()
    for row in range(dev_rows):
        total = mixed[batches - 1, row]
        for batch in range(batches - 1):
            total = total + from_y[batch, row]
        out_ref[:, row, :] = total
    for copy in pending:
        copy.wait_send()


def per_device(peer_count, node_count, columns, pencil_e, pencil_a, precond, neighbours):
    dev_rows, _, block, _ = pencil_e.shape
    col_count = columns.shape[0]
    batches = node_count // 2
    width = col_count // batches
    chunk = width // 2
    entries = dev_rows * SLOTS
    half, full = jnp.bfloat16, jnp.float32
    vmem = pl.BlockSpec(memory_space=pltpu.VMEM)
    anywhere = pl.BlockSpec(memory_space=pl.ANY)
    dma = pltpu.SemaphoreType.DMA
    crossings = max(batches - 1, 1)
    scratch = [
        pltpu.VMEM((entries, block, 2 * block), half),
        pltpu.VMEM((dev_rows, block, 2 * block), half),
        pltpu.VMEM((col_count, dev_rows, block), full),
        pltpu.VMEM((8, 128), jnp.int32),
        pltpu.VMEM((LANES + 2, 8, 128), jnp.int32),
        pltpu.SMEM((LANES + 2, 8, 128), jnp.int32),
        pltpu.VMEM((LANES, 8, 128), jnp.int32),
        pltpu.VMEM((LANES, 8, 128), jnp.int32),
        pltpu.SMEM((LANES, 8, 128), jnp.int32),
        pltpu.VMEM((dev_rows + 1, col_count, block), half),
        pltpu.VMEM((batches, HALO, width, block), half),
        pltpu.VMEM((batches, HALO, width, block), half),
        pltpu.VMEM((dev_rows, col_count, block), full),
        pltpu.VMEM((batches, HALO + 1, width, block), full),
        pltpu.VMEM((batches, dev_rows, width, block), full),
        pltpu.VMEM((SWEEPS, dev_rows + 1, 2 * col_count, block), half),
        pltpu.VMEM((SWEEPS, batches, HALO, 2 * width, block), half),
        pltpu.VMEM((SWEEPS, batches, HALO, 2 * width, block), half),
        pltpu.VMEM((dev_rows, 2 * col_count, 2 * block), full),
        pltpu.VMEM((batches, HALO + 1, 2 * width, 2 * block), full),
        pltpu.VMEM((batches, dev_rows, 2 * width, block), full),
        pltpu.VMEM((batches, 2, dev_rows, 2 * chunk, block), full),
        pltpu.VMEM((batches, dev_rows, 2 * chunk, block), full),
        pltpu.VMEM((batches, dev_rows, 2 * chunk, block), full),
        pltpu.VMEM((crossings, dev_rows, 2 * chunk, block), full),
        dma((4,)),
        dma,
        dma,
        dma((LANES,)),
        dma((LANES,)),
        dma(((1 + SWEEPS) * batches, LANES)),
        dma(((1 + SWEEPS) * batches, LANES)),
        dma((batches,)),
        dma((batches,)),
        dma((crossings,)),
        dma((crossings,)),
    ]
    summed = pl.pallas_call(
        functools.partial(kernel, peer_count, node_count),
        out_shape=jax.ShapeDtypeStruct((2 * chunk, dev_rows, block), full),
        in_specs=[vmem, vmem, anywhere, anywhere, anywhere],
        out_specs=vmem,
        scratch_shapes=scratch,
        compiler_params=pltpu.CompilerParams(
            collective_id=0, has_side_effects=True, vmem_limit_bytes=60 * 1024 * 1024
        ),
    )(
        neighbours.T,
        columns,
        pencil_e.reshape(entries, block, block),
        pencil_a.reshape(entries, block, block),
        precond.reshape(2, dev_rows, block, block),
    )
    return summed.reshape(2, chunk, dev_rows, block) * (1.0 / node_count)


def solution(mesh):
    placed = (
        P(None, "rows", None),
        P("rows", None, None, None),
        P("rows", None, None, None),
        P("node", None, "rows", None, None),
        P("rows", None),
    )
    return jax.shard_map(
        functools.partial(per_device, mesh.shape["rows"], mesh.shape["node"]),
        mesh=mesh,
        in_specs=placed,
        out_specs=P(None, "node", "rows", None),
        check_vma=False,
    )
```

```python
import functools
import math

import jax
import jax.numpy as jnp
from jax import lax
from jax.experimental import pallas as pl
from jax.experimental.pallas import tpu as pltpu
from jax.sharding import PartitionSpec as P

SLOTS = 5
HMAX = 6
REACH = 2
SWEEPS = 2
LANES = 2 * REACH + 1
HALO = LANES * HMAX
MESH = pl.DeviceIdType.MESH
ROW_STEP = 8


def lane_offsets(peer_count):
    return list(range(-REACH, 0)) + list(range(1, REACH + 1)) + [peer_count // 2]


def lane_sum(value):
    shift = value.shape[1] // 2
    while shift:
        value = value + pltpu.roll(value, shift, 1)
        shift //= 2
    return value


def index_tables(neighbours, dev_rows, me, owners):
    wide = 128
    entries = dev_rows * SLOTS
    position = lax.broadcasted_iota(jnp.int32, (8, wide), 1)
    sub = lax.broadcasted_iota(jnp.int32, (8, wide), 0)
    flat = jnp.zeros((8, wide), jnp.int32)
    slot_of = jnp.zeros((8, wide), jnp.int32)
    for slot in range(SLOTS):
        line = jnp.broadcast_to(neighbours[slot : slot + 1, :], (8, wide))
        flat = flat + (pltpu.roll(line, slot * dev_rows, 1) if slot else line)
        if slot:
            slot_of = slot_of + (position >= slot * dev_rows).astype(jnp.int32)
    row_of = position - slot_of * dev_rows
    first = jnp.zeros((8, wide), jnp.int32)
    for lane, owner in enumerate(owners):
        first = jnp.where(sub == lane, owner * dev_rows, first)
    inside = (flat >= first) & (flat < first + dev_rows) & (sub < LANES) & (position < entries)
    count = jnp.where(inside, 1, 0)
    shift = 1
    while shift < wide:
        count = count + jnp.where(position >= shift, pltpu.roll(count, shift, 1), 0)
        shift *= 2
    rank = count - 1

    def over_lanes(value):
        value = jnp.where(inside, value, 0)
        for step in (4, 2, 1):
            value = value + pltpu.roll(value, step, 0)
        return value

    remote = over_lanes(jnp.ones_like(flat)) > 0
    arrived = jnp.clip(jnp.where(remote, over_lanes(sub * HMAX + rank), HALO), 0, HALO)
    place = jnp.where(remote, over_lanes(sub * 8 + rank), -1)
    local = flat - over_lanes(first)
    own = jnp.clip(jnp.where(remote, dev_rows, flat - me * dev_rows), 0, dev_rows)
    entry_of = row_of * SLOTS + slot_of
    entry, wanted = [], []
    for lane in range(LANES):
        matched = place == sub + lane * 8
        entry.append(jnp.clip(lane_sum(jnp.where(matched, entry_of, 0)), 0, entries - 1))
        wanted.append(jnp.clip(lane_sum(jnp.where(matched, local, 0)), 0, dev_rows - 1))
    return own, arrived, entry, wanted


def kernel(
    peer_count,
    node_count,
    near_ref,
    cols_ref,
    e_ref,
    a_ref,
    p_ref,
    out_ref,
    weights,
    inverse,
    wide_cols,
    near,
    table_v,
    table_s,
    want_v,
    asked_v,
    asked_s,
    vec_0,
    send_0,
    halo_0,
    part_0,
    prod_0,
    rhs,
    vec,
    outgoing,
    halo,
    part,
    prod,
    iterate,
    share,
    from_core,
    mixed,
    from_y,
    load_sem,
    table_sem,
    asked_sem,
    want_send,
    want_recv,
    halo_send,
    halo_recv,
    core_send,
    core_recv,
    y_send,
    y_recv,
):
    batches, dev_rows, width, block = rhs.shape
    chunk = width // 2
    offsets = lane_offsets(peer_count)
    me = lax.axis_index("rows")
    node = lax.axis_index("node")
    my_y = node // 2
    my_core = node % 2

    def batch_y(batch):
        return lax.rem(my_y + 1 + batch, batches)

    load_e = pltpu.make_async_copy(e_ref, weights.at[:, :, 0:block], load_sem.at[0])
    load_a = pltpu.make_async_copy(a_ref, weights.at[:, :, block : 2 * block], load_sem.at[1])
    load_p = [
        pltpu.make_async_copy(
            p_ref.at[index], inverse.at[:, :, index * block : (index + 1) * block], load_sem.at[2 + index]
        )
        for index in range(2)
    ]
    for copy in [load_e] + load_p + [load_a]:
        copy.start()

    def behind(offset):
        return lax.rem(me + offset + peer_count, peer_count)

    barrier = pltpu.get_barrier_semaphore()
    for offset in offsets:
        pl.semaphore_signal(barrier, inc=1, device_id={"rows": behind(offset)}, device_id_type=MESH)
    for step in range(1, node_count):
        other = lax.rem(node + step, node_count)
        pl.semaphore_signal(barrier, inc=1, device_id={"node": other}, device_id_type=MESH)

    near[...] = jnp.zeros(near.shape, near.dtype)
    near[0:SLOTS, 0:dev_rows] = near_ref[...]
    own, arrived, entry, wanted = index_tables(
        near[...], dev_rows, me, [behind(offset) for offset in offsets]
    )
    for lane in range(LANES):
        want_v[lane] = wanted[lane]
        table_v[lane] = entry[lane]
    table_v[LANES] = own
    table_v[LANES + 1] = arrived
    to_table = pltpu.make_async_copy(table_v, table_s, table_sem)
    to_table.start()

    pl.semaphore_wait(barrier, LANES + node_count - 1)

    pending = []
    for lane, offset in enumerate(offsets):
        copy = pltpu.make_async_remote_copy(
            src_ref=want_v.at[lane],
            dst_ref=asked_v.at[lane],
            send_sem=want_send.at[lane],
            recv_sem=want_recv.at[lane],
            device_id={"rows": behind(offset)},
            device_id_type=MESH,
        )
        copy.start()
        pending.append(copy)
    wide_cols[...] = cols_ref[...].astype(jnp.float32)
    for row in range(dev_rows):
        for batch in range(batches):
            at = pl.multiple_of(batch_y(batch) * width, width)
            vec_0[row, batch * width : (batch + 1) * width] = wide_cols[pl.ds(at, width), row, :].astype(
                jnp.bfloat16
            )
    vec_0[dev_rows] = jnp.zeros(vec_0.shape[1:], vec_0.dtype)
    for batch in range(batches):
        prod_0[batch, HALO] = jnp.zeros(prod_0.shape[2:], prod_0.dtype)
        prod[batch, HALO] = jnp.zeros(prod.shape[2:], prod.dtype)
    for sweep in range(SWEEPS):
        vec[sweep, dev_rows] = jnp.zeros(vec.shape[2:], vec.dtype)

    for copy in pending:
        copy.wait_recv()
    to_scalars = pltpu.make_async_copy(asked_v, asked_s, asked_sem)
    to_scalars.start()
    to_scalars.wait()
    to_table.wait()

    def send_halo(phase, source, batch, rows, leaving, arriving):
        copies = [None] * LANES
        for lane in (4, 0, 3, 1, 2):
            for rank in range(HMAX):
                leaving[lane * HMAX + rank] = source[
                    asked_s[lane, rank, 0], batch * rows : (batch + 1) * rows
                ]
            here = pl.ds(lane * HMAX, HMAX)
            copy = pltpu.make_async_remote_copy(
                src_ref=leaving.at[here],
                dst_ref=arriving.at[here],
                send_sem=halo_send.at[phase, lane],
                recv_sem=halo_recv.at[phase, lane],
                device_id={"rows": behind(-offsets[lane])},
                device_id_type=MESH,
            )
            copy.start()
            copies[lane] = copy
            pending.append(copy)
        return copies

    def row_loop(body):
        def step_rows(step, carry):
            for inner in range(ROW_STEP):
                body(step * ROW_STEP + inner)
            return carry

        lax.fori_loop(0, dev_rows // ROW_STEP, step_rows, 0)

    def own_products(source, columns, target):
        def one_row(row):
            at = row * SLOTS
            picked = [source[table_s[LANES, 0, slot * dev_rows + row]] for slot in range(SLOTS)]
            matrix = weights[pl.ds(at, SLOTS), :, 0:columns].reshape(SLOTS * block, columns)
            target[row] = jnp.dot(
                jnp.concatenate(picked, axis=1), matrix, preferred_element_type=jnp.float32
            )

        row_loop(one_row)

    def halo_products(copies, arriving, columns, target):
        for lane in (1, 2, 0, 3, 4):
            copies[lane].wait_recv()

            for rank in range(HMAX):
                at = lane * HMAX + rank
                matrix = weights[table_s[lane, rank, 0], :, 0:columns]
                target[at] = jnp.dot(arriving[at], matrix, preferred_element_type=jnp.float32)

    def all_products(row, target, batch, rows, halo_target):
        summed = target[row, batch * rows : (batch + 1) * rows]
        for slot in range(1, SLOTS):
            summed = summed + halo_target[table_s[LANES + 1, 0, slot * dev_rows + row]]
        return summed

    node_real = jnp.float32(0.0)
    node_imag = jnp.float32(0.0)
    for index in range(node_count):
        angle = 2.0 * math.pi * (index + 0.5) / node_count
        node_real = jnp.where(node == index, jnp.float32(math.cos(angle)), node_real)
        node_imag = jnp.where(node == index, jnp.float32(math.sin(angle)), node_imag)

    def phase_of(sweep, batch):
        return (1 + sweep) * batches + batch

    flights = {}
    for batch in range(batches):
        flights[-1, batch] = send_halo(
            phase_of(-1, batch), vec_0, batch, width, send_0.at[batch], halo_0.at[batch]
        )
    load_e.wait()
    own_products(vec_0, block, part_0)
    load_a.wait()
    for copy in load_p:
        copy.wait()

    for batch in range(batches):
        halo_products(flights[-1, batch], halo_0.at[batch], block, prod_0.at[batch])

        def first_rows(row, batch=batch):
            right = all_products(row, part_0, batch, width, prod_0.at[batch])
            rhs[batch, row] = right
            both = jnp.dot(
                right.astype(jnp.bfloat16), inverse[row], preferred_element_type=jnp.float32
            )
            fresh = jnp.concatenate([both[:, 0:block], both[:, block:]], axis=0)
            iterate[batch, row] = fresh
            vec[0, row, batch * 2 * width : (batch + 1) * 2 * width] = fresh.astype(jnp.bfloat16)

        row_loop(first_rows)
        flights[0, batch] = send_halo(
            phase_of(0, batch), vec.at[0], batch, 2 * width, outgoing.at[0, batch], halo.at[0, batch]
        )

    core_copies = []
    y_copies = []

    def finish_core(batch):
        for copy in core_copies[batch]:
            copy.wait_recv()
        mixed[batch] = share[batch, my_core] + from_core[batch]
        if batch < batches - 1:
            copy = pltpu.make_async_remote_copy(
                src_ref=mixed.at[batch],
                dst_ref=from_y.at[batch],
                send_sem=y_send.at[batch],
                recv_sem=y_recv.at[batch],
                device_id={"node": 2 * batch_y(batch) + my_core},
                device_id_type=MESH,
            )
            copy.start()
            y_copies.append(copy)
            pending.append(copy)

    for sweep in range(SWEEPS):
        own_products(vec.at[sweep], 2 * block, part)
        for batch in range(batches):
            arriving, halo_target = halo.at[sweep, batch], prod.at[batch]
            if sweep == SWEEPS - 1 and batch > 0:
                finish_core(batch - 1)
            halo_products(flights[sweep, batch], arriving, 2 * block, halo_target)

            def sweep_rows(row, sweep=sweep, batch=batch, halo_target=halo_target):
                both = all_products(row, part, batch, 2 * width, halo_target)
                e_real, a_real = both[:width, :block], both[:width, block:]
                e_imag, a_imag = both[width:, :block], both[width:, block:]
                right = rhs[batch, row]
                res_real = right - (node_real * e_real - node_imag * e_imag - a_real)
                res_imag = -(node_real * e_imag + node_imag * e_real - a_imag)
                residual = jnp.concatenate([res_real, res_imag], axis=0).astype(jnp.bfloat16)
                moved = jnp.dot(residual, inverse[row], preferred_element_type=jnp.float32)
                real = iterate[batch, row, 0:width] + (
                    moved[:width, :block] - moved[width:, block:]
                )
                imag = iterate[batch, row, width : 2 * width] + (
                    moved[:width, block:] + moved[width:, :block]
                )
                if sweep < SWEEPS - 1:
                    iterate[batch, row, 0:width] = real
                    iterate[batch, row, width : 2 * width] = imag
                    vec[sweep + 1, row, batch * 2 * width : (batch + 1) * 2 * width] = (
                        jnp.concatenate([real, imag], axis=0).astype(jnp.bfloat16)
                    )
                else:
                    out_real = node_real * real - node_imag * imag
                    out_imag = node_real * imag + node_imag * real
                    for core in range(2):
                        at = core * chunk
                        share[batch, core, row, 0:chunk] = out_real[at : at + chunk]
                        share[batch, core, row, chunk : 2 * chunk] = out_imag[at : at + chunk]

            if sweep == SWEEPS - 1:
                core_copies.append([])
            for third in range(dev_rows // ROW_STEP):
                for inner in range(ROW_STEP):
                    sweep_rows(third * ROW_STEP + inner)
                if sweep == SWEEPS - 1:
                    here = pl.ds(third * ROW_STEP, ROW_STEP)
                    copy = pltpu.make_async_remote_copy(
                        src_ref=share.at[batch, 1 - my_core, here],
                        dst_ref=from_core.at[batch, here],
                        send_sem=core_send.at[batch, third],
                        recv_sem=core_recv.at[batch, third],
                        device_id={"node": 2 * my_y + (1 - my_core)},
                        device_id_type=MESH,
                    )
                    copy.start()
                    core_copies[batch].append(copy)
                    pending.append(copy)
            if sweep < SWEEPS - 1:
                flights[sweep + 1, batch] = send_halo(
                    phase_of(sweep + 1, batch),
                    vec.at[sweep + 1],
                    batch,
                    2 * width,
                    outgoing.at[sweep + 1, batch],
                    halo.at[sweep + 1, batch],
                )

    finish_core(batches - 1)
    for copy in y_copies:
        copy.wait_recv()
    for row in range(dev_rows):
        total = mixed[batches - 1, row]
        for batch in range(batches - 1):
            total = total + from_y[batch, row]
        out_ref[:, row, :] = total
    for copy in pending:
        copy.wait_send()


def per_device(peer_count, node_count, columns, pencil_e, pencil_a, precond, neighbours):
    dev_rows, _, block, _ = pencil_e.shape
    col_count = columns.shape[0]
    batches = node_count // 2
    width = col_count // batches
    chunk = width // 2
    entries = dev_rows * SLOTS
    half, full = jnp.bfloat16, jnp.float32
    vmem = pl.BlockSpec(memory_space=pltpu.VMEM)
    anywhere = pl.BlockSpec(memory_space=pl.ANY)
    dma = pltpu.SemaphoreType.DMA
    crossings = max(batches - 1, 1)
    scratch = [
        pltpu.VMEM((entries, block, 2 * block), half),
        pltpu.VMEM((dev_rows, block, 2 * block), half),
        pltpu.VMEM((col_count, dev_rows, block), full),
        pltpu.VMEM((8, 128), jnp.int32),
        pltpu.VMEM((LANES + 2, 8, 128), jnp.int32),
        pltpu.SMEM((LANES + 2, 8, 128), jnp.int32),
        pltpu.VMEM((LANES, 8, 128), jnp.int32),
        pltpu.VMEM((LANES, 8, 128), jnp.int32),
        pltpu.SMEM((LANES, 8, 128), jnp.int32),
        pltpu.VMEM((dev_rows + 1, col_count, block), half),
        pltpu.VMEM((batches, HALO, width, block), half),
        pltpu.VMEM((batches, HALO, width, block), half),
        pltpu.VMEM((dev_rows, col_count, block), full),
        pltpu.VMEM((batches, HALO + 1, width, block), full),
        pltpu.VMEM((batches, dev_rows, width, block), full),
        pltpu.VMEM((SWEEPS, dev_rows + 1, 2 * col_count, block), half),
        pltpu.VMEM((SWEEPS, batches, HALO, 2 * width, block), half),
        pltpu.VMEM((SWEEPS, batches, HALO, 2 * width, block), half),
        pltpu.VMEM((dev_rows, 2 * col_count, 2 * block), full),
        pltpu.VMEM((batches, HALO + 1, 2 * width, 2 * block), full),
        pltpu.VMEM((batches, dev_rows, 2 * width, block), full),
        pltpu.VMEM((batches, 2, dev_rows, 2 * chunk, block), full),
        pltpu.VMEM((batches, dev_rows, 2 * chunk, block), full),
        pltpu.VMEM((batches, dev_rows, 2 * chunk, block), full),
        pltpu.VMEM((crossings, dev_rows, 2 * chunk, block), full),
        dma((4,)),
        dma,
        dma,
        dma((LANES,)),
        dma((LANES,)),
        dma(((1 + SWEEPS) * batches, LANES)),
        dma(((1 + SWEEPS) * batches, LANES)),
        dma((batches, dev_rows // ROW_STEP)),
        dma((batches, dev_rows // ROW_STEP)),
        dma((crossings,)),
        dma((crossings,)),
    ]
    summed = pl.pallas_call(
        functools.partial(kernel, peer_count, node_count),
        out_shape=jax.ShapeDtypeStruct((2 * chunk, dev_rows, block), full),
        in_specs=[vmem, vmem, anywhere, anywhere, anywhere],
        out_specs=vmem,
        scratch_shapes=scratch,
        compiler_params=pltpu.CompilerParams(
            collective_id=0, has_side_effects=True, vmem_limit_bytes=60 * 1024 * 1024
        ),
    )(
        neighbours.T,
        columns,
        pencil_e.reshape(entries, block, block),
        pencil_a.reshape(entries, block, block),
        precond.reshape(2, dev_rows, block, block),
    )
    return summed.reshape(2, chunk, dev_rows, block) * (1.0 / node_count)


def solution(mesh):
    placed = (
        P(None, "rows", None),
        P("rows", None, None, None),
        P("rows", None, None, None),
        P("node", None, "rows", None, None),
        P("rows", None),
    )
    return jax.shard_map(
        functools.partial(per_device, mesh.shape["rows"], mesh.shape["node"]),
        mesh=mesh,
        in_specs=placed,
        out_specs=P(None, "node", "rows", None),
        check_vma=False,
    )
```

```python
import functools
import math

import jax
import jax.numpy as jnp
from jax import lax
from jax.experimental import pallas as pl
from jax.experimental.pallas import tpu as pltpu
from jax.sharding import PartitionSpec as P

SLOTS = 5
HMAX = 6
REACH = 2
SWEEPS = 2
LANES = 2 * REACH + 1
HALO = LANES * HMAX
MESH = pl.DeviceIdType.MESH
ROW_STEP = 8


def lane_offsets(peer_count):
    return list(range(-REACH, 0)) + list(range(1, REACH + 1)) + [peer_count // 2]


def lane_sum(value):
    shift = value.shape[1] // 2
    while shift:
        value = value + pltpu.roll(value, shift, 1)
        shift //= 2
    return value


def index_tables(neighbours, dev_rows, me, owners):
    wide = 128
    entries = dev_rows * SLOTS
    position = lax.broadcasted_iota(jnp.int32, (8, wide), 1)
    sub = lax.broadcasted_iota(jnp.int32, (8, wide), 0)
    flat = jnp.zeros((8, wide), jnp.int32)
    slot_of = jnp.zeros((8, wide), jnp.int32)
    for slot in range(SLOTS):
        line = jnp.broadcast_to(neighbours[slot : slot + 1, :], (8, wide))
        flat = flat + (pltpu.roll(line, slot * dev_rows, 1) if slot else line)
        if slot:
            slot_of = slot_of + (position >= slot * dev_rows).astype(jnp.int32)
    row_of = position - slot_of * dev_rows
    first = jnp.zeros((8, wide), jnp.int32)
    for lane, owner in enumerate(owners):
        first = jnp.where(sub == lane, owner * dev_rows, first)
    inside = (flat >= first) & (flat < first + dev_rows) & (sub < LANES) & (position < entries)
    count = jnp.where(inside, 1, 0)
    shift = 1
    while shift < wide:
        count = count + jnp.where(position >= shift, pltpu.roll(count, shift, 1), 0)
        shift *= 2
    rank = count - 1

    def over_lanes(value):
        value = jnp.where(inside, value, 0)
        for step in (4, 2, 1):
            value = value + pltpu.roll(value, step, 0)
        return value

    remote = over_lanes(jnp.ones_like(flat)) > 0
    arrived = jnp.clip(jnp.where(remote, over_lanes(sub * HMAX + rank), HALO), 0, HALO)
    place = jnp.where(remote, over_lanes(sub * 8 + rank), -1)
    local = flat - over_lanes(first)
    own = jnp.clip(jnp.where(remote, dev_rows, flat - me * dev_rows), 0, dev_rows)
    entry_of = row_of * SLOTS + slot_of
    entry, wanted = [], []
    for lane in range(LANES):
        matched = place == sub + lane * 8
        entry.append(jnp.clip(lane_sum(jnp.where(matched, entry_of, 0)), 0, entries - 1))
        wanted.append(jnp.clip(lane_sum(jnp.where(matched, local, 0)), 0, dev_rows - 1))
    return own, arrived, entry, wanted


def kernel(
    peer_count,
    node_count,
    near_ref,
    cols_ref,
    e_ref,
    a_ref,
    p_ref,
    out_ref,
    weights,
    inverse,
    wide_cols,
    near,
    table_v,
    table_s,
    want_v,
    asked_v,
    asked_s,
    vec_0,
    send_0,
    halo_0,
    part_0,
    prod_0,
    rhs,
    vec,
    outgoing,
    halo,
    part,
    prod,
    iterate,
    share,
    from_core,
    mixed,
    from_y,
    load_sem,
    table_sem,
    asked_sem,
    want_send,
    want_recv,
    halo_send,
    halo_recv,
    core_send,
    core_recv,
    y_send,
    y_recv,
):
    batches, dev_rows, width, block = rhs.shape
    chunk = width // 2
    offsets = lane_offsets(peer_count)
    me = lax.axis_index("rows")
    node = lax.axis_index("node")
    my_y = node // 2
    my_core = node % 2

    def batch_y(batch):
        return lax.rem(my_y + 1 + batch, batches)

    load_e = pltpu.make_async_copy(e_ref, weights.at[:, :, 0:block], load_sem.at[0])
    load_a = pltpu.make_async_copy(a_ref, weights.at[:, :, block : 2 * block], load_sem.at[1])
    load_p = [
        pltpu.make_async_copy(
            p_ref.at[index], inverse.at[:, :, index * block : (index + 1) * block], load_sem.at[2 + index]
        )
        for index in range(2)
    ]
    for copy in [load_e] + load_p + [load_a]:
        copy.start()

    def behind(offset):
        return lax.rem(me + offset + peer_count, peer_count)

    barrier = pltpu.get_barrier_semaphore()
    for offset in offsets:
        pl.semaphore_signal(barrier, inc=1, device_id={"rows": behind(offset)}, device_id_type=MESH)
    for step in range(1, node_count):
        other = lax.rem(node + step, node_count)
        pl.semaphore_signal(barrier, inc=1, device_id={"node": other}, device_id_type=MESH)

    near[...] = jnp.zeros(near.shape, near.dtype)
    near[0:SLOTS, 0:dev_rows] = near_ref[...]
    own, arrived, entry, wanted = index_tables(
        near[...], dev_rows, me, [behind(offset) for offset in offsets]
    )
    for lane in range(LANES):
        want_v[lane] = wanted[lane]
        table_v[lane] = entry[lane]
    table_v[LANES] = own
    table_v[LANES + 1] = arrived
    to_table = pltpu.make_async_copy(table_v, table_s, table_sem)
    to_table.start()

    pl.semaphore_wait(barrier, LANES + node_count - 1)

    pending = []
    for lane, offset in enumerate(offsets):
        copy = pltpu.make_async_remote_copy(
            src_ref=want_v.at[lane],
            dst_ref=asked_v.at[lane],
            send_sem=want_send.at[lane],
            recv_sem=want_recv.at[lane],
            device_id={"rows": behind(offset)},
            device_id_type=MESH,
        )
        copy.start()
        pending.append(copy)
    wide_cols[...] = cols_ref[...].astype(jnp.float32)
    for row in range(dev_rows):
        for batch in range(batches):
            at = pl.multiple_of(batch_y(batch) * width, width)
            vec_0[row, batch * width : (batch + 1) * width] = wide_cols[pl.ds(at, width), row, :].astype(
                jnp.bfloat16
            )
    vec_0[dev_rows] = jnp.zeros(vec_0.shape[1:], vec_0.dtype)
    for batch in range(batches):
        prod_0[batch, HALO] = jnp.zeros(prod_0.shape[2:], prod_0.dtype)
        prod[batch, HALO] = jnp.zeros(prod.shape[2:], prod.dtype)
    for sweep in range(SWEEPS):
        vec[sweep, dev_rows] = jnp.zeros(vec.shape[2:], vec.dtype)

    for copy in pending:
        copy.wait_recv()
    to_scalars = pltpu.make_async_copy(asked_v, asked_s, asked_sem)
    to_scalars.start()
    to_scalars.wait()
    to_table.wait()

    def send_halo(phase, source, batch, rows, leaving, arriving):
        copies = [None] * LANES
        for lane in (4, 0, 3, 1, 2):
            for rank in range(HMAX):
                leaving[lane * HMAX + rank] = source[
                    asked_s[lane, rank, 0], batch * rows : (batch + 1) * rows
                ]
            here = pl.ds(lane * HMAX, HMAX)
            copy = pltpu.make_async_remote_copy(
                src_ref=leaving.at[here],
                dst_ref=arriving.at[here],
                send_sem=halo_send.at[phase, lane],
                recv_sem=halo_recv.at[phase, lane],
                device_id={"rows": behind(-offsets[lane])},
                device_id_type=MESH,
            )
            copy.start()
            copies[lane] = copy
            pending.append(copy)
        return copies

    def row_loop(body):
        def step_rows(step, carry):
            for inner in range(ROW_STEP):
                body(step * ROW_STEP + inner)
            return carry

        lax.fori_loop(0, dev_rows // ROW_STEP, step_rows, 0)

    def own_products(source, columns, target):
        def one_row(row):
            at = row * SLOTS
            picked = [source[table_s[LANES, 0, slot * dev_rows + row]] for slot in range(SLOTS)]
            matrix = weights[pl.ds(at, SLOTS), :, 0:columns].reshape(SLOTS * block, columns)
            target[row] = jnp.dot(
                jnp.concatenate(picked, axis=1), matrix, preferred_element_type=jnp.float32
            )

        row_loop(one_row)

    def halo_products(copies, arriving, columns, target):
        for lane in (1, 2, 0, 3, 4):
            copies[lane].wait_recv()

            for rank in range(HMAX):
                at = lane * HMAX + rank
                matrix = weights[table_s[lane, rank, 0], :, 0:columns]
                target[at] = jnp.dot(arriving[at], matrix, preferred_element_type=jnp.float32)

    def all_products(row, target, batch, rows, halo_target):
        summed = target[row, batch * rows : (batch + 1) * rows]
        for slot in range(1, SLOTS):
            summed = summed + halo_target[table_s[LANES + 1, 0, slot * dev_rows + row]]
        return summed

    node_real = jnp.float32(0.0)
    node_imag = jnp.float32(0.0)
    for index in range(node_count):
        angle = 2.0 * math.pi * (index + 0.5) / node_count
        node_real = jnp.where(node == index, jnp.float32(math.cos(angle)), node_real)
        node_imag = jnp.where(node == index, jnp.float32(math.sin(angle)), node_imag)

    def phase_of(sweep, batch):
        return (1 + sweep) * batches + batch

    flights = {}
    for batch in range(batches):
        flights[-1, batch] = send_halo(
            phase_of(-1, batch), vec_0, batch, width, send_0.at[batch], halo_0.at[batch]
        )
    load_e.wait()
    own_products(vec_0, block, part_0)
    load_a.wait()
    for copy in load_p:
        copy.wait()

    for batch in range(batches):
        halo_products(flights[-1, batch], halo_0.at[batch], block, prod_0.at[batch])

        def first_rows(row, batch=batch):
            right = all_products(row, part_0, batch, width, prod_0.at[batch])
            rhs[batch, row] = right
            both = jnp.dot(
                right.astype(jnp.bfloat16), inverse[row], preferred_element_type=jnp.float32
            )
            fresh = jnp.concatenate([both[:, 0:block], both[:, block:]], axis=0)
            iterate[batch, row] = fresh
            vec[0, row, batch * 2 * width : (batch + 1) * 2 * width] = fresh.astype(jnp.bfloat16)

        row_loop(first_rows)
        flights[0, batch] = send_halo(
            phase_of(0, batch), vec.at[0], batch, 2 * width, outgoing.at[0, batch], halo.at[0, batch]
        )

    core_copies = []
    y_copies = []

    def finish_core(batch):
        for copy in core_copies[batch]:
            copy.wait_recv()
        mixed[batch] = share[batch, my_core] + from_core[batch]
        if batch < batches - 1:
            copy = pltpu.make_async_remote_copy(
                src_ref=mixed.at[batch],
                dst_ref=from_y.at[batch],
                send_sem=y_send.at[batch],
                recv_sem=y_recv.at[batch],
                device_id={"node": 2 * batch_y(batch) + my_core},
                device_id_type=MESH,
            )
            copy.start()
            y_copies.append(copy)
            pending.append(copy)

    for sweep in range(SWEEPS):
        own_products(vec.at[sweep], 2 * block, part)
        for batch in range(batches):
            arriving, halo_target = halo.at[sweep, batch], prod.at[batch]
            if sweep == SWEEPS - 1 and batch > 0:
                finish_core(batch - 1)
            halo_products(flights[sweep, batch], arriving, 2 * block, halo_target)

            def sweep_rows(row, sweep=sweep, batch=batch, halo_target=halo_target):
                both = all_products(row, part, batch, 2 * width, halo_target)
                e_real, a_real = both[:width, :block], both[:width, block:]
                e_imag, a_imag = both[width:, :block], both[width:, block:]
                right = rhs[batch, row]
                res_real = right - (node_real * e_real - node_imag * e_imag - a_real)
                res_imag = -(node_real * e_imag + node_imag * e_real - a_imag)
                residual = jnp.concatenate([res_real, res_imag], axis=0).astype(jnp.bfloat16)
                moved = jnp.dot(residual, inverse[row], preferred_element_type=jnp.float32)
                real = iterate[batch, row, 0:width] + (
                    moved[:width, :block] - moved[width:, block:]
                )
                imag = iterate[batch, row, width : 2 * width] + (
                    moved[:width, block:] + moved[width:, :block]
                )
                if sweep < SWEEPS - 1:
                    iterate[batch, row, 0:width] = real
                    iterate[batch, row, width : 2 * width] = imag
                    vec[sweep + 1, row, batch * 2 * width : (batch + 1) * 2 * width] = (
                        jnp.concatenate([real, imag], axis=0).astype(jnp.bfloat16)
                    )
                else:
                    out_real = node_real * real - node_imag * imag
                    out_imag = node_real * imag + node_imag * real
                    for core in range(2):
                        at = core * chunk
                        share[batch, core, row, 0:chunk] = out_real[at : at + chunk]
                        share[batch, core, row, chunk : 2 * chunk] = out_imag[at : at + chunk]

            if sweep == SWEEPS - 1:
                core_copies.append([])
            for third in range(dev_rows // ROW_STEP):
                for inner in range(ROW_STEP):
                    sweep_rows(third * ROW_STEP + inner)
                if sweep == SWEEPS - 1:
                    here = pl.ds(third * ROW_STEP, ROW_STEP)
                    copy = pltpu.make_async_remote_copy(
                        src_ref=share.at[batch, 1 - my_core, here],
                        dst_ref=from_core.at[batch, here],
                        send_sem=core_send.at[batch, third],
                        recv_sem=core_recv.at[batch, third],
                        device_id={"node": 2 * my_y + (1 - my_core)},
                        device_id_type=MESH,
                    )
                    copy.start()
                    core_copies[batch].append(copy)
                    pending.append(copy)
            if sweep < SWEEPS - 1:
                flights[sweep + 1, batch] = send_halo(
                    phase_of(sweep + 1, batch),
                    vec.at[sweep + 1],
                    batch,
                    2 * width,
                    outgoing.at[sweep + 1, batch],
                    halo.at[sweep + 1, batch],
                )

    finish_core(batches - 1)
    for copy in y_copies:
        copy.wait_recv()
    for row in range(dev_rows):
        total = mixed[batches - 1, row]
        for batch in range(batches - 1):
            total = total + from_y[batch, row]
        out_ref[:, row, :] = total
    for copy in pending:
        copy.wait_send()


def per_device(peer_count, node_count, columns, pencil_e, pencil_a, precond, neighbours):
    dev_rows, _, block, _ = pencil_e.shape
    col_count = columns.shape[0]
    batches = node_count // 2
    width = col_count // batches
    chunk = width // 2
    entries = dev_rows * SLOTS
    half, full = jnp.bfloat16, jnp.float32
    vmem = pl.BlockSpec(memory_space=pltpu.VMEM)
    anywhere = pl.BlockSpec(memory_space=pl.ANY)
    dma = pltpu.SemaphoreType.DMA
    crossings = max(batches - 1, 1)
    scratch = [
        pltpu.VMEM((entries, block, 2 * block), half),
        pltpu.VMEM((dev_rows, block, 2 * block), half),
        pltpu.VMEM((col_count, dev_rows, block), full),
        pltpu.VMEM((8, 128), jnp.int32),
        pltpu.VMEM((LANES + 2, 8, 128), jnp.int32),
        pltpu.SMEM((LANES + 2, 8, 128), jnp.int32),
        pltpu.VMEM((LANES, 8, 128), jnp.int32),
        pltpu.VMEM((LANES, 8, 128), jnp.int32),
        pltpu.SMEM((LANES, 8, 128), jnp.int32),
        pltpu.VMEM((dev_rows + 1, col_count, block), half),
        pltpu.VMEM((batches, HALO, width, block), half),
        pltpu.VMEM((batches, HALO, width, block), half),
        pltpu.VMEM((dev_rows, col_count, block), full),
        pltpu.VMEM((batches, HALO + 1, width, block), full),
        pltpu.VMEM((batches, dev_rows, width, block), full),
        pltpu.VMEM((SWEEPS, dev_rows + 1, 2 * col_count, block), half),
        pltpu.VMEM((SWEEPS, batches, HALO, 2 * width, block), half),
        pltpu.VMEM((SWEEPS, batches, HALO, 2 * width, block), half),
        pltpu.VMEM((dev_rows, 2 * col_count, 2 * block), full),
        pltpu.VMEM((batches, HALO + 1, 2 * width, 2 * block), full),
        pltpu.VMEM((batches, dev_rows, 2 * width, block), full),
        pltpu.VMEM((batches, 2, dev_rows, 2 * chunk, block), full),
        pltpu.VMEM((batches, dev_rows, 2 * chunk, block), full),
        pltpu.VMEM((batches, dev_rows, 2 * chunk, block), full),
        pltpu.VMEM((crossings, dev_rows, 2 * chunk, block), full),
        dma((4,)),
        dma,
        dma,
        dma((LANES,)),
        dma((LANES,)),
        dma(((1 + SWEEPS) * batches, LANES)),
        dma(((1 + SWEEPS) * batches, LANES)),
        dma((batches, dev_rows // ROW_STEP)),
        dma((batches, dev_rows // ROW_STEP)),
        dma((crossings,)),
        dma((crossings,)),
    ]
    summed = pl.pallas_call(
        functools.partial(kernel, peer_count, node_count),
        out_shape=jax.ShapeDtypeStruct((2 * chunk, dev_rows, block), full),
        in_specs=[vmem, vmem, anywhere, anywhere, anywhere],
        out_specs=vmem,
        scratch_shapes=scratch,
        compiler_params=pltpu.CompilerParams(
            collective_id=0, has_side_effects=True, vmem_limit_bytes=53 * 1024 * 1024
        ),
    )(
        neighbours.T,
        columns,
        pencil_e.reshape(entries, block, block),
        pencil_a.reshape(entries, block, block),
        precond.reshape(2, dev_rows, block, block),
    )
    return summed.reshape(2, chunk, dev_rows, block) * (1.0 / node_count)


def solution(mesh):
    placed = (
        P(None, "rows", None),
        P("rows", None, None, None),
        P("rows", None, None, None),
        P("node", None, "rows", None, None),
        P("rows", None),
    )
    return jax.shard_map(
        functools.partial(per_device, mesh.shape["rows"], mesh.shape["node"]),
        mesh=mesh,
        in_specs=placed,
        out_specs=P(None, "node", "rows", None),
        check_vma=False,
    )
```
